256 devices in a mesh: head: 4 (over z_lo), ctx: 64 (over z_hi, x, y, core).
Axes of the slice: x: 4, y: 4, z: 8 (z_hi: 2, z_lo: 4; z = z_hi * 4 + z_lo), core: 2. Of those that a mesh axis runs over, the one named last changes fastest.
Arguments:
- query_rows: bfloat16 [24576, 5120], P(('ctx', 'head')), may hold values from -26 to 26
- key_rows: bfloat16 [24576, 5120], P(('ctx', 'head')), may hold values from -26 to 26
- value_rows: bfloat16 [24576, 5120], P(('ctx', 'head')), may hold values from -6 to 6
- block_mask: int32 [40, 192, 192], P('head', 'ctx'), may hold values from 0 to 1
- head_type: int32 [40], P('head'), may hold values from 0 to 1
Outputs:
- attended: bfloat16 [24576, 5120], P(('ctx', 'head'))
The draws below stay inside these ranges and needn't reach their ends.
All inputs are finite; a program needn't handle non-finite values.
Results may differ from the reference program's by a relative error of at most 0.0044.
Values may be sent and summed in bfloat16 or wider, within the bound.
A program may use at most 64 MiB of HBM per device.

```python
import jax
import jax.numpy as jnp
from jax import lax

HEADS = 40
HEAD_DIM = 128
BLOCK = 128
TOK_CTX = 384
REACH = 4
TOKENS = 24576


def shared_parts(key):
    shape = (TOKENS, HEADS * HEAD_DIM)
    pattern = jnp.clip(jax.random.normal(jax.random.fold_in(key, 11), shape, jnp.float32), -3.0, 3.0)
    return pattern


def draw_query_rows(key, part):
    pattern = shared_parts(key)
    key = jax.random.fold_in(key, 1)
    rows = 1.6 * jax.random.normal(key, pattern.shape, jnp.float32)
    return rows.astype(jnp.bfloat16)


def draw_key_rows(key, part):
    pattern = shared_parts(key)
    key = jax.random.fold_in(key, 2)
    rows = 1.6 * jax.random.normal(key, pattern.shape, jnp.float32)
    return rows.astype(jnp.bfloat16)


def draw_block_mask(key, part):
    key = jax.random.fold_in(key, 5)
    tiles = TOKENS // BLOCK
    levels = jax.random.randint(jax.random.fold_in(key, 1), (HEADS, tiles, 1), 1, 8)
    raw = jax.random.randint(jax.random.fold_in(key, 2), (HEADS, tiles, tiles), 0, 8)
    return (raw < levels).astype(jnp.int32)


def place_ends(entries, key, low, largest):
    dims = entries.shape
    place = [jax.random.randint(jax.random.fold_in(key, axis), (), 0, dims[axis]) for axis in range(len(dims))]
    entries = entries.at[tuple(place)].set(low)
    longest = dims.index(max(dims))
    place[longest] = (place[longest] + 1) % dims[longest]
    return entries.at[tuple(place)].set(largest)


def block_scale(stream_key, dims, split, smallest, high):
    def one(dim, parts):
        draws = jax.random.uniform(jax.random.fold_in(jax.random.fold_in(stream_key, 6), dim), (parts,), jnp.float32, smallest / len(split), high / len(split))
        return jnp.repeat(jnp.exp(draws), dims[dim] // parts).reshape((-1,) + (1,) * (len(dims) - dim - 1))

    loudness = one(*split[0])
    for cut in split[1:]:
        loudness = loudness * one(*cut)
    return loudness


def noise(own_key, extent, scale, bound, cuts=(), kind=jnp.bfloat16):
    drawn = jax.random.normal(own_key, extent, jnp.float32) * scale
    if len(cuts) > 0:
        drawn = block_scale(own_key, extent, cuts, -0.22, 0.18) * drawn
    return jnp.clip(drawn, min=-bound, max=bound).astype(kind)


def setup_inputs(seed: int = 0) -> dict:
    keys = jax.random.split(jax.random.key(seed), 6)
    query_rows = draw_query_rows(jax.random.fold_in(keys[5], 71), 0)
    key_rows = draw_key_rows(jax.random.fold_in(keys[5], 71), 0)
    value_rows = noise(keys[2], (TOKENS, HEADS * HEAD_DIM), 1.0, 6.0, ((0, 256),))
    block_mask = draw_block_mask(jax.random.fold_in(keys[5], 71), 0)
    head_type = place_ends(jax.random.randint(keys[4], (HEADS,), 0, 2), jax.random.fold_in(keys[4], 1), 0, 1).astype(jnp.int32)
    return dict(query_rows=query_rows, key_rows=key_rows, value_rows=value_rows, block_mask=block_mask, head_type=head_type)


masked_score = -1e30


def reference(query_rows, key_rows, value_rows, block_mask, head_type):
    blocks = TOKENS // BLOCK
    per_dev = TOK_CTX // BLOCK
    far_limit = REACH * per_dev
    window = 2 * far_limit + 1
    scale = HEAD_DIM ** -0.5
    limits = jnp.where(head_type == 1, far_limit, per_dev).astype(jnp.int32)
    query_tiles = query_rows.reshape(blocks, BLOCK, HEADS, HEAD_DIM)
    padding = ((far_limit, far_limit), (0, 0), (0, 0), (0, 0))
    key_tiles = jnp.pad(key_rows.reshape(blocks, BLOCK, HEADS, HEAD_DIM), padding)
    value_tiles = jnp.pad(value_rows.reshape(blocks, BLOCK, HEADS, HEAD_DIM), padding)
    mask_padded = jnp.pad(block_mask, ((0, 0), (0, 0), (far_limit, far_limit)))

    def one_block(index):
        queries = query_tiles[index].astype(jnp.float32)
        near_keys = lax.dynamic_slice_in_dim(key_tiles, index, window, 0).astype(jnp.float32)
        near_values = lax.dynamic_slice_in_dim(value_tiles, index, window, 0).astype(jnp.float32)
        tile_row = lax.dynamic_slice_in_dim(mask_padded[:, index, :], index, window, 1)
        key_blocks = index - far_limit + jnp.arange(window, dtype=jnp.int32)
        inside = (key_blocks >= 0) & (key_blocks < blocks)
        distance = jnp.abs(key_blocks - index)
        allowed = ((tile_row == 1) | (distance == 0)[None, :]) & inside[None, :] & (distance[None, :] <= limits[:, None])
        scores = jnp.einsum("qhd,wkhd->hqwk", queries, near_keys) * scale
        scores = jnp.where(allowed[:, None, :, None], scores, masked_score)
        best = jnp.max(scores, axis=(2, 3), keepdims=True)
        raw = jnp.where(allowed[:, None, :, None], jnp.exp(scores - best), 0.0)
        total = jnp.sum(raw, axis=(2, 3))
        rounded = lax.optimization_barrier(raw.astype(jnp.bfloat16))
        weights = rounded.astype(jnp.float32)
        mixed = jnp.einsum("hqwk,wkhd->qhd", weights, near_values) / jnp.transpose(total)[:, :, None]
        return mixed.astype(jnp.bfloat16)

    result = lax.map(one_block, jnp.arange(blocks, dtype=jnp.int32))
    return result.reshape(TOKENS, HEADS * HEAD_DIM)
```

```python
import math

import jax
import jax.numpy as jnp
from jax import lax
from jax.experimental import pallas as pl
from jax.experimental.pallas import tpu as pltpu
from jax.sharding import PartitionSpec as P

MESH = pl.DeviceIdType.MESH
TILE = 128
DIM = 128
HEADS = 5
ROWS = 96
CHUNK = 768
TILES = CHUNK // TILE
REACH = 12
NEAR = 3
SPAN = 2 * REACH + 1
KEYS = SPAN * TILE
WINDOW = 5 * CHUNK
OWN = 2 * CHUNK
CHUNKS = 32
FLAG_ROWS = 16
LOW = 1e30
RATE = math.log2(math.e) / math.sqrt(DIM)


def wait_for(ref, sem):
    pltpu.make_async_copy(ref, ref, sem).wait()


def kernel(
    q_ref, k_ref, v_ref, flag_ref, o_ref,
    kv, qb, ob, flags, bias,
    kv_send, q_send, flag_send, o_send, y_send,
    kv_recv, q_recv, flag_recv, o_recv, near_recv, far_recv,
):
    hd = lax.axis_index("head")
    ctx = lax.axis_index("ctx")
    zh = ctx // 32
    xy = (ctx // 2) % 16
    core = ctx % 2
    z = zh * 4 + hd
    chunk = core * 16 + xy
    loops = zh == core
    has_left = chunk > 0
    has_right = chunk < CHUNKS - 1

    def at(z_, xy_, core_):
        return {"head": z_ % 4, "ctx": (z_ // 4) * 32 + xy_ * 2 + core_}

    left = at(z, (chunk + CHUNKS - 1) % 16, ((chunk + CHUNKS - 1) % CHUNKS) // 16)
    right = at(z, (chunk + 1) % 16, ((chunk + 1) % CHUNKS) // 16)

    barrier = pltpu.get_barrier_semaphore()

    def greet(n, carry):
        other = (z * 2 + core + n) % 16
        pl.semaphore_signal(barrier, inc=1, device_id=at(other // 2, xy, other % 2), device_id_type=MESH)
        return carry

    lax.fori_loop(1, 16, greet, 0)

    @pl.when(has_left)
    def _():
        pl.semaphore_signal(barrier, inc=1, device_id=left, device_id_type=MESH)

    @pl.when(has_right)
    def _():
        pl.semaphore_signal(barrier, inc=1, device_id=right, device_id_type=MESH)

    pl.semaphore_wait(barrier, 15 + has_left.astype(jnp.int32) + has_right.astype(jnp.int32))

    mine = core * 384 + hd * ROWS

    def parts(i, z_):
        cols = pl.ds(pl.multiple_of((z_ * HEADS + i) * DIM, DIM), DIM)
        rows = pl.ds(pl.multiple_of(OWN + mine, 16), ROWS)
        q_rows = pl.ds(pl.multiple_of(mine, 16), ROWS)
        return (
            (k_ref.at[:, cols], kv.at[i, 0, rows, :], kv_send, kv_recv.at[i]),
            (v_ref.at[:, cols], kv.at[i, 1, rows, :], kv_send, kv_recv.at[i]),
            (q_ref.at[:, cols], qb.at[i, q_rows, :], q_send, q_recv.at[i]),
        )

    def push(src, dst, send, recv, to):
        pltpu.make_async_remote_copy(
            src_ref=src, dst_ref=dst, send_sem=send, recv_sem=recv, device_id=to, device_id_type=MESH
        ).start()

    def spread(i, carry):
        def one(j, inner):
            half = j // 2 + 1
            step = jnp.where(j % 2 == 0, half, 8 - half)
            z_ = (z + step) % 8
            for src, dst, send, recv in parts(i, z_):
                push(src, dst, send, recv, at(z_, xy, zh))
            return inner

        lax.fori_loop(0, 7, one, 0)

        @pl.when(loops)
        def _():
            for src, dst, send, recv in parts(i, z):
                pltpu.make_async_copy(src, dst, recv).start()

        @pl.when(jnp.logical_not(loops))
        def _():
            for src, dst, send, recv in parts(i, z):
                push(src, dst, send, recv, at(z, xy, zh))

        return carry

    lax.fori_loop(0, HEADS, spread, 0)

    for e in range(2):
        z_ = 2 * hd + e
        here = jnp.logical_and(loops, z_ == z)

        @pl.when(here)
        def _():
            pltpu.make_async_copy(flag_ref.at[e], flags.at[core], flag_recv).start()

        @pl.when(jnp.logical_not(here))
        def _():
            push(flag_ref.at[e], flags.at[core], flag_send.at[e], flag_recv, at(z_, xy, zh))

    def clear(slot, when):
        @pl.when(when)
        def _():
            def one(i, carry):
                kv[i, :, pl.ds(slot * CHUNK, CHUNK), :] = jnp.zeros((2, CHUNK, DIM), jnp.bfloat16)
                return carry

            lax.fori_loop(0, HEADS, one, 0)

    clear(0, chunk < 2)
    clear(1, chunk < 1)
    clear(3, chunk > CHUNKS - 2)
    clear(4, chunk > CHUNKS - 3)

    wait_for(flags, flag_recv)
    spots = lax.broadcasted_iota(jnp.int32, (TILE, KEYS), 1) // TILE
    rows_ = lax.broadcasted_iota(jnp.int32, (TILE, KEYS), 0)
    wide = (spots == rows_).astype(jnp.bfloat16)
    for c in range(2):
        seen = jnp.dot(flags[c].astype(jnp.bfloat16), wide, preferred_element_type=jnp.float32)
        bias[c] = (seen - 1.0) * LOW

    def slot(i, s):
        return kv.at[i, :, pl.ds(s * CHUNK, CHUNK), :]

    def send_own(i):
        wait_for(slot(i, 2), kv_recv.at[i])

        @pl.when(has_right)
        def _():
            push(slot(i, 2), slot(i, 1), y_send.at[0], near_recv.at[0, i], right)

        @pl.when(has_left)
        def _():
            push(slot(i, 2), slot(i, 3), y_send.at[1], near_recv.at[1, i], left)

    def pass_on(i):
        @pl.when(has_left)
        def _():
            wait_for(slot(i, 1), near_recv.at[0, i])

            @pl.when(has_right)
            def _():
                push(slot(i, 1), slot(i, 0), y_send.at[2], far_recv.at[0, i], right)

        @pl.when(has_right)
        def _():
            wait_for(slot(i, 3), near_recv.at[1, i])

            @pl.when(has_left)
            def _():
                push(slot(i, 3), slot(i, 4), y_send.at[3], far_recv.at[1, i], left)

    def attend(i):
        wait_for(qb.at[i], q_recv.at[i])

        @pl.when(chunk >= 2)
        def _():
            wait_for(slot(i, 0), far_recv.at[0, i])

        @pl.when(chunk < CHUNKS - 2)
        def _():
            wait_for(slot(i, 4), far_recv.at[1, i])

        def tile(a, carry):
            start = pl.multiple_of(a * TILE, TILE)
            q = qb[i, pl.ds(start, TILE), :]
            keys = kv[i, 0, pl.ds(start, KEYS), :]
            s = lax.dot_general(q, keys, (((1,), (1,)), ((), ())), preferred_element_type=jnp.float32)
            s = s + bias[a // 3, pl.ds(i * 3 + a % 3, 1), :]
            best = jnp.max(s, axis=1, keepdims=True)
            raw = jnp.exp2((s - best) * RATE)
            total = jnp.sum(raw, axis=1, keepdims=True)
            values = kv[i, 1, pl.ds(start, KEYS), :]
            mixed = jnp.dot(raw.astype(jnp.bfloat16), values, preferred_element_type=jnp.float32)
            ob[i, pl.ds(start, TILE), :] = (mixed / total).astype(jnp.bfloat16)
            return carry

        lax.fori_loop(0, TILES, tile, 0)

        cols = pl.ds(pl.multiple_of((z * HEADS + i) * DIM, DIM), DIM)

        def owner(n):
            zl = (hd + n // 2) % 4
            cs = (core + n) % 2
            return ob.at[i, pl.ds(pl.multiple_of(cs * 384 + zl * ROWS, 16), ROWS), :], at(core * 4 + zl, xy, cs)

        @pl.when(loops)
        def _():
            pltpu.make_async_copy(owner(0)[0], o_ref.at[:, cols], o_recv).start()

        @pl.when(jnp.logical_not(loops))
        def _():
            push(owner(0)[0], o_ref.at[:, cols], o_send, o_recv, owner(0)[1])

        def one(n, carry):
            src, to = owner(n)
            push(src, o_ref.at[:, cols], o_send, o_recv, to)
            return carry

        lax.fori_loop(1, 8, one, 0)

    for step in range(HEADS + 2):
        if step < HEADS:
            send_own(step)
        if 1 <= step <= HEADS:
            pass_on(step - 1)
        if step >= 2:
            attend(step - 2)

    wait_for(o_ref, o_recv)

    def sent(rows):
        wait_for(kv.at[:, :, pl.ds(0, rows), :], kv_send)
        wait_for(qb.at[:, pl.ds(0, rows), :], q_send)
        wait_for(ob.at[:, pl.ds(0, rows), :], o_send)

    @pl.when(loops)
    def _():
        sent(CHUNK - ROWS)

    @pl.when(jnp.logical_not(loops))
    def _():
        sent(CHUNK)

    for e in range(2):

        @pl.when(jnp.logical_not(jnp.logical_and(loops, 2 * hd + e == z)))
        def _():
            wait_for(flag_ref.at[e], flag_send.at[e])

    whole = kv.at[:, :, pl.ds(0, CHUNK), :]

    @pl.when(has_right)
    def _():
        wait_for(whole, y_send.at[0])

        @pl.when(has_left)
        def _():
            wait_for(whole, y_send.at[2])

    @pl.when(has_left)
    def _():
        wait_for(whole, y_send.at[1])

        @pl.when(has_right)
        def _():
            wait_for(whole, y_send.at[3])


def per_device(query_rows, key_rows, value_rows, block_mask, head_type):
    ctx = lax.axis_index("ctx")
    heads, tiles, count = block_mask.shape
    padded = jnp.pad(block_mask, ((0, 0), (0, 0), (REACH, REACH)))
    near = lax.dynamic_slice_in_dim(padded, ctx * tiles, SPAN + tiles - 1, 2)
    seen = jnp.stack([near[:, t, t : t + SPAN] for t in range(tiles)], axis=1)
    distance = jnp.abs(jnp.arange(SPAN, dtype=jnp.int32) - REACH)
    limit = jnp.where(head_type == 1, REACH, NEAR).astype(jnp.int32)
    allowed = ((seen == 1) | (distance == 0)) & (distance <= limit[:, None, None])
    flags = allowed.astype(jnp.float32).reshape(2, HEADS * tiles, SPAN)
    flags = jnp.pad(flags, ((0, 0), (0, FLAG_ROWS - HEADS * tiles), (0, TILE - SPAN)))
    any_ = pl.BlockSpec(memory_space=pl.ANY)
    dma = pltpu.SemaphoreType.DMA
    return pl.pallas_call(
        kernel,
        out_shape=jax.ShapeDtypeStruct(query_rows.shape, jnp.bfloat16),
        in_specs=[any_] * 4,
        out_specs=any_,
        scratch_shapes=[
            pltpu.VMEM((HEADS, 2, WINDOW, DIM), jnp.bfloat16),
            pltpu.VMEM((HEADS, CHUNK, DIM), jnp.bfloat16),
            pltpu.VMEM((HEADS, CHUNK, DIM), jnp.bfloat16),
            pltpu.VMEM((2, FLAG_ROWS, TILE), jnp.float32),
            pltpu.VMEM((2, FLAG_ROWS, KEYS), jnp.float32),
            dma, dma, dma((2,)), dma, dma((4,)),
            dma((HEADS,)), dma((HEADS,)), dma, dma, dma((2, HEADS)), dma((2, HEADS)),
        ],
        compiler_params=pltpu.CompilerParams(
            collective_id=0, has_side_effects=True, vmem_limit_bytes=48 * 1024 * 1024
        ),
    )(query_rows, key_rows, value_rows, flags)


def solution(mesh):
    placed = (
        P(("ctx", "head"), None),
        P(("ctx", "head"), None),
        P(("ctx", "head"), None),
        P("head", "ctx", None),
        P("head"),
    )
    return jax.shard_map(
        per_device, mesh=mesh, in_specs=placed, out_specs=P(("ctx", "head"), None), check_vma=False
    )
```

```python
import math

import jax
import jax.numpy as jnp
from jax import lax
from jax.experimental import pallas as pl
from jax.experimental.pallas import tpu as pltpu
from jax.sharding import PartitionSpec as P

MESH = pl.DeviceIdType.MESH
TILE = 128
DIM = 128
HEADS = 5
ROWS = 96
CHUNK = 768
TILES = CHUNK // TILE
REACH = 12
NEAR = 3
PAIR = 2 * TILE
SPAN = 2 * REACH + 2
KEYS = SPAN * TILE
STEP = 256
UNITS = 2 * HEADS
WINDOW = 5 * CHUNK
OWN = 2 * CHUNK
CHUNKS = 32
FLAG_ROWS = 16
LOW = 1e30
RATE = math.log2(math.e) / math.sqrt(DIM)


def wait_for(ref, sem):
    pltpu.make_async_copy(ref, ref, sem).wait()


def kernel(
    q_ref, k_ref, v_ref, flag_ref, o_ref,
    kv, qb, ob, flags, bias, held,
    kv_send, q_send, flag_send, o_send, y_send,
    kv_recv, q_recv, flag_recv, o_recv, near_recv, far_recv,
):
    hd = lax.axis_index("head")
    ctx = lax.axis_index("ctx")
    zh = ctx // 32
    xy = (ctx // 2) % 16
    core = ctx % 2
    z = zh * 4 + hd
    chunk = core * 16 + xy
    loops = zh == core
    has_left = chunk > 0
    has_right = chunk < CHUNKS - 1

    def at(z_, xy_, core_):
        return {"head": z_ % 4, "ctx": (z_ // 4) * 32 + xy_ * 2 + core_}

    left = at(z, (chunk + CHUNKS - 1) % 16, ((chunk + CHUNKS - 1) % CHUNKS) // 16)
    right = at(z, (chunk + 1) % 16, ((chunk + 1) % CHUNKS) // 16)

    barrier = pltpu.get_barrier_semaphore()

    def greet(n, carry):
        other = (z * 2 + core + n) % 16
        pl.semaphore_signal(barrier, inc=1, device_id=at(other // 2, xy, other % 2), device_id_type=MESH)
        return carry

    lax.fori_loop(1, 16, greet, 0)

    @pl.when(has_left)
    def _():
        pl.semaphore_signal(barrier, inc=1, device_id=left, device_id_type=MESH)

    @pl.when(has_right)
    def _():
        pl.semaphore_signal(barrier, inc=1, device_id=right, device_id_type=MESH)

    pl.semaphore_wait(barrier, 15 + has_left.astype(jnp.int32) + has_right.astype(jnp.int32))

    mine = core * 384 + hd * ROWS

    def parts(i, z_):
        cols = pl.ds(pl.multiple_of((z_ * HEADS + i) * DIM, DIM), DIM)
        rows = pl.ds(pl.multiple_of(OWN + mine, 16), ROWS)
        q_rows = pl.ds(pl.multiple_of(mine, 16), ROWS)
        return (
            (k_ref.at[:, cols], kv.at[2 * i, rows, :], kv_send, kv_recv.at[2 * i]),
            (v_ref.at[:, cols], kv.at[2 * i + 1, rows, :], kv_send, kv_recv.at[2 * i + 1]),
            (q_ref.at[:, cols], qb.at[i, q_rows, :], q_send, q_recv.at[i]),
        )

    def push(src, dst, send, recv, to):
        pltpu.make_async_remote_copy(
            src_ref=src, dst_ref=dst, send_sem=send, recv_sem=recv, device_id=to, device_id_type=MESH
        ).start()

    def spread(i, kind):
        def one(j, carry):
            half = j // 2 + 1
            step = jnp.where(j % 2 == 0, half, 8 - half)
            z_ = (z + step) % 8
            src, dst, send, recv = parts(i, z_)[kind]
            push(src, dst, send, recv, at(z_, xy, zh))
            return carry

        lax.fori_loop(0, 7, one, 0)

        @pl.when(loops)
        def _():
            src, dst, send, recv = parts(i, z)[kind]
            pltpu.make_async_copy(src, dst, recv).start()

        @pl.when(jnp.logical_not(loops))
        def _():
            src, dst, send, recv = parts(i, z)[kind]
            push(src, dst, send, recv, at(z, xy, zh))

    spread(0, 0)
    spread(0, 1)

    for e in range(2):
        z_ = 2 * hd + e
        here = jnp.logical_and(loops, z_ == z)

        @pl.when(here)
        def _():
            pltpu.make_async_copy(flag_ref.at[e], flags.at[core], flag_recv).start()

        @pl.when(jnp.logical_not(here))
        def _():
            push(flag_ref.at[e], flags.at[core], flag_send.at[e], flag_recv, at(z_, xy, zh))

    def clear(slot, when):
        @pl.when(when)
        def _():
            def one(i, carry):
                kv[i, pl.ds(slot * CHUNK, CHUNK), :] = jnp.zeros((CHUNK, DIM), jnp.bfloat16)
                return carry

            lax.fori_loop(0, UNITS, one, 0)

    clear(0, chunk < 2)
    clear(1, chunk < 1)
    clear(3, chunk > CHUNKS - 2)
    clear(4, chunk > CHUNKS - 3)

    wait_for(flags, flag_recv)
    spots = lax.broadcasted_iota(jnp.int32, (TILE, KEYS), 1) // TILE
    rows_ = lax.broadcasted_iota(jnp.int32, (TILE, KEYS), 0)
    wide = (spots == rows_).astype(jnp.bfloat16)
    for c in range(2):
        seen = jnp.dot(flags[c].astype(jnp.bfloat16), wide, preferred_element_type=jnp.float32)
        seen = (seen - 1.0) * LOW
        for i in range(HEADS):
            bias[pl.ds(i * TILES + 3 * c, 3), :] = seen[3 * i : 3 * i + 3]

    def slot(i, s):
        return kv.at[i, pl.ds(s * CHUNK, CHUNK), :]

    def send_own(i):
        wait_for(slot(i, 2), kv_recv.at[i])

        @pl.when(has_right)
        def _():
            push(slot(i, 2), slot(i, 1), y_send.at[0], near_recv.at[0, i], right)

        @pl.when(has_left)
        def _():
            push(slot(i, 2), slot(i, 3), y_send.at[1], near_recv.at[1, i], left)

    def pass_on(i):
        @pl.when(has_left)
        def _():
            wait_for(slot(i, 1), near_recv.at[0, i])

            @pl.when(has_right)
            def _():
                push(slot(i, 1), slot(i, 0), y_send.at[2], far_recv.at[0, i], right)

        @pl.when(has_right)
        def _():
            wait_for(slot(i, 3), near_recv.at[1, i])

            @pl.when(has_left)
            def _():
                push(slot(i, 3), slot(i, 4), y_send.at[3], far_recv.at[1, i], left)

    def attend(i):
        wait_for(qb.at[i], q_recv.at[i])
        for u in (2 * i, 2 * i + 1):

            @pl.when(chunk >= 2)
            def _():
                wait_for(slot(u, 0), far_recv.at[0, u])

            @pl.when(chunk < CHUNKS - 2)
            def _():
                wait_for(slot(u, 4), far_recv.at[1, u])

        for p in range(CHUNK // PAIR):
            start = p * PAIR
            q = qb[i, pl.ds(start, PAIR), :]
            best = jnp.full((PAIR, TILE), -3e38, jnp.float32)
            for j in range(0, KEYS, STEP):
                keys = kv[2 * i, pl.ds(start + j, STEP), :]
                s = lax.dot_general(q, keys, (((1,), (1,)), ((), ())), preferred_element_type=jnp.float32)
                even = s[:TILE] + bias[pl.ds(i * TILES + 2 * p, 1), pl.ds(j, STEP)]
                odd = s[TILE:] + bias[pl.ds(i * TILES + 2 * p + 1, 1), pl.ds(j, STEP)]
                s = jnp.concatenate([even, odd], axis=0)
                held[p, :, pl.ds(j, STEP)] = s
                for t in range(0, STEP, TILE):
                    best = jnp.maximum(best, s[:, t : t + TILE])
            best = jnp.max(best, axis=1, keepdims=True)
            total = jnp.zeros((PAIR, TILE), jnp.float32)
            mixed = jnp.zeros((PAIR, DIM), jnp.float32)
            for j in range(0, KEYS, STEP):
                raw = jnp.exp2((held[p, :, pl.ds(j, STEP)] - best) * RATE)
                for t in range(0, STEP, TILE):
                    total = total + raw[:, t : t + TILE]
                values = kv[2 * i + 1, pl.ds(start + j, STEP), :]
                mixed = mixed + jnp.dot(raw.astype(jnp.bfloat16), values, preferred_element_type=jnp.float32)
            total = jnp.sum(total, axis=1, keepdims=True)
            ob[i, pl.ds(start, PAIR), :] = (mixed / total).astype(jnp.bfloat16)

        cols = pl.ds(pl.multiple_of((z * HEADS + i) * DIM, DIM), DIM)

        def owner(n):
            zl = (hd + n // 2) % 4
            cs = (core + n) % 2
            return ob.at[i, pl.ds(pl.multiple_of(cs * 384 + zl * ROWS, 16), ROWS), :], at(core * 4 + zl, xy, cs)

        @pl.when(loops)
        def _():
            pltpu.make_async_copy(owner(0)[0], o_ref.at[:, cols], o_recv).start()

        @pl.when(jnp.logical_not(loops))
        def _():
            push(owner(0)[0], o_ref.at[:, cols], o_send, o_recv, owner(0)[1])

        def one(n, carry):
            src, to = owner(n)
            push(src, o_ref.at[:, cols], o_send, o_recv, to)
            return carry

        lax.fori_loop(1, 8, one, 0)

    def advance(s, carry):
        @pl.when(s < HEADS)
        def _():
            for t in range(2):
                send_own(2 * s + t)

                @pl.when(s < HEADS - 1)
                def _():
                    spread(s + 1, t)

                if t == 1:

                    @pl.when(s >= 1)
                    def _():
                        spread(s - 1, 2)

                    @pl.when(s == HEADS - 1)
                    def _():
                        spread(s, 2)

                    pass_on(2 * s)
                else:

                    @pl.when(s >= 1)
                    def _():
                        pass_on(2 * s - 1)

        @pl.when(s == HEADS)
        def _():
            pass_on(UNITS - 1)

        @pl.when(s >= 2)
        def _():
            attend(s - 2)

        return carry

    lax.fori_loop(0, HEADS + 2, advance, 0)

    wait_for(o_ref, o_recv)

    def sent(rows):
        wait_for(kv.at[:, pl.ds(0, rows), :], kv_send)
        wait_for(qb.at[:, pl.ds(0, rows), :], q_send)
        wait_for(ob.at[:, pl.ds(0, rows), :], o_send)

    @pl.when(loops)
    def _():
        sent(CHUNK - ROWS)

    @pl.when(jnp.logical_not(loops))
    def _():
        sent(CHUNK)

    for e in range(2):

        @pl.when(jnp.logical_not(jnp.logical_and(loops, 2 * hd + e == z)))
        def _():
            wait_for(flag_ref.at[e], flag_send.at[e])

    whole = kv.at[:, pl.ds(0, CHUNK), :]

    @pl.when(has_right)
    def _():
        wait_for(whole, y_send.at[0])

        @pl.when(has_left)
        def _():
            wait_for(whole, y_send.at[2])

    @pl.when(has_left)
    def _():
        wait_for(whole, y_send.at[1])

        @pl.when(has_right)
        def _():
            wait_for(whole, y_send.at[3])


def per_device(query_rows, key_rows, value_rows, block_mask, head_type):
    ctx = lax.axis_index("ctx")
    heads, tiles, count = block_mask.shape
    padded = jnp.pad(block_mask, ((0, 0), (0, 0), (REACH + 1, REACH + 1)))
    base = ctx * tiles
    shift = (base + jnp.arange(tiles, dtype=jnp.int32)) % 2
    near = lax.dynamic_slice_in_dim(padded, base, SPAN + tiles, 2)
    seen = jnp.stack(
        [jnp.where(shift[t] == 1, near[:, t, t : t + SPAN], near[:, t, t + 1 : t + 1 + SPAN]) for t in range(tiles)],
        axis=1,
    )
    distance = jnp.abs(jnp.arange(SPAN, dtype=jnp.int32) - REACH - shift[:, None])
    limit = jnp.where(head_type == 1, REACH, NEAR).astype(jnp.int32)
    allowed = ((seen == 1) | (distance == 0)) & (distance <= limit[:, None, None])
    flags = allowed.astype(jnp.float32).reshape(2, HEADS * tiles, SPAN)
    flags = jnp.pad(flags, ((0, 0), (0, FLAG_ROWS - HEADS * tiles), (0, TILE - SPAN)))
    any_ = pl.BlockSpec(memory_space=pltpu.HBM)
    dma = pltpu.SemaphoreType.DMA
    return pl.pallas_call(
        kernel,
        out_shape=jax.ShapeDtypeStruct(query_rows.shape, jnp.bfloat16),
        in_specs=[any_] * 4,
        out_specs=any_,
        scratch_shapes=[
            pltpu.VMEM((UNITS, WINDOW, DIM), jnp.bfloat16),
            pltpu.VMEM((HEADS, CHUNK, DIM), jnp.bfloat16),
            pltpu.VMEM((HEADS, CHUNK, DIM), jnp.bfloat16),
            pltpu.VMEM((2, FLAG_ROWS, TILE), jnp.float32),
            pltpu.VMEM((HEADS * TILES + 2, KEYS), jnp.float32),
            pltpu.VMEM((CHUNK // PAIR, PAIR, KEYS), jnp.float32),
            dma, dma, dma((2,)), dma, dma((4,)),
            dma((UNITS,)), dma((HEADS,)), dma, dma, dma((2, UNITS)), dma((2, UNITS)),
        ],
        compiler_params=pltpu.CompilerParams(
            collective_id=0, has_side_effects=True, vmem_limit_bytes=56 * 1024 * 1024
        ),
    )(query_rows, key_rows, value_rows, flags)


def solution(mesh):
    placed = (
        P(("ctx", "head"), None),
        P(("ctx", "head"), None),
        P(("ctx", "head"), None),
        P("head", "ctx", None),
        P("head"),
    )
    return jax.shard_map(
        per_device, mesh=mesh, in_specs=placed, out_specs=P(("ctx", "head"), None), check_vma=False
    )
```

```python
import math

import jax
import jax.numpy as jnp
from jax import lax
from jax.experimental import pallas as pl
from jax.experimental.pallas import tpu as pltpu
from jax.sharding import PartitionSpec as P

MESH = pl.DeviceIdType.MESH
TILE = 128
DIM = 128
HEADS = 5
ROWS = 96
CHUNK = 768
TILES = CHUNK // TILE
REACH = 12
NEAR = 3
PAIR = 2 * TILE
SPAN = 2 * REACH + 2
KEYS = SPAN * TILE
STEP = 256
UNITS = 2 * HEADS
PIECES = 3 * HEADS
FIRST = 2
LEAD = 3
WINDOW = 5 * CHUNK
OWN = 2 * CHUNK
CHUNKS = 32
RING = 4
FLAG_ROWS = 16
COUNT = 192
LOW = 1e30
RATE = math.log2(math.e) / math.sqrt(DIM)


def wait_for(ref, sem):
    pltpu.make_async_copy(ref, ref, sem).wait()


def kernel(
    q_ref, k_ref, v_ref, mask_ref, type_ref, o_ref,
    kv, qb, ob, masks, lines, shown, flags, bias, held, weights, totals,
    mask_copy, kv_send, q_send, flag_send, o_send, y_send,
    kv_recv, q_recv, flag_recv, o_recv, near_recv, far_recv,
):
    hd = lax.axis_index("head")
    ctx = lax.axis_index("ctx")
    zh = ctx // 32
    xy = (ctx // 2) % 16
    core = ctx % 2
    z = zh * 4 + hd
    chunk = core * 16 + xy
    loops = zh == core
    has_left = chunk > 0
    has_right = chunk < CHUNKS - 1

    def at(z_, xy_, core_):
        return {"head": z_ % 4, "ctx": (z_ // 4) * 32 + xy_ * 2 + core_}

    def beside(by):
        other = (chunk + by + CHUNKS) % CHUNKS
        return at(z, other % 16, other // 16)

    left, right = beside(-1), beside(1)
    back, ahead = beside(-RING), beside(RING)
    y = xy % RING
    first_row = chunk < RING
    last_row = chunk >= CHUNKS - RING
    at_start, at_end = y == 0, y == RING - 1
    inside = jnp.logical_not(jnp.logical_or(at_start, at_end))
    closing = beside(jnp.where(at_start, RING - 1, 1 - RING))

    barrier = pltpu.get_barrier_semaphore()

    def greet(n, carry):
        other = (z * 2 + core + n) % 16
        pl.semaphore_signal(barrier, inc=1, device_id=at(other // 2, xy, other % 2), device_id_type=MESH)
        return carry

    lax.fori_loop(1, 16, greet, 0)

    has_back, has_ahead = jnp.logical_not(first_row), jnp.logical_not(last_row)
    has_closing = jnp.logical_not(inside)
    partners = ((has_left, left), (has_right, right), (has_back, back), (has_ahead, ahead), (has_closing, closing))
    for there, partner in partners:

        @pl.when(there)
        def _():
            pl.semaphore_signal(barrier, inc=1, device_id=partner, device_id_type=MESH)

    pl.semaphore_wait(barrier, 15 + sum(there.astype(jnp.int32) for there, _ in partners))

    mine = core * 384 + hd * ROWS

    fetch = pltpu.make_async_copy(mask_ref, masks, mask_copy)
    fetch.start()

    def parts(i, z_):
        cols = pl.ds(pl.multiple_of((z_ * HEADS + i) * DIM, DIM), DIM)
        rows = pl.ds(pl.multiple_of(OWN + mine, 16), ROWS)
        q_rows = pl.ds(pl.multiple_of(mine, 16), ROWS)
        return (
            (k_ref.at[:, cols], kv.at[2 * i, rows, :], kv_send.at[2 * i], kv_recv.at[2 * i]),
            (v_ref.at[:, cols], kv.at[2 * i + 1, rows, :], kv_send.at[2 * i + 1], kv_recv.at[2 * i + 1]),
            (q_ref.at[:, cols], qb.at[i, q_rows, :], q_send, q_recv.at[i]),
        )

    def push(src, dst, send, recv, to):
        pltpu.make_async_remote_copy(
            src_ref=src, dst_ref=dst, send_sem=send, recv_sem=recv, device_id=to, device_id_type=MESH
        ).start()

    def spread(i, kind):
        def one(j, carry):
            half = j // 2 + 1
            step = jnp.where(j % 2 == 0, half, 8 - half)
            z_ = (z + step) % 8
            src, dst, send, recv = parts(i, z_)[kind]
            push(src, dst, send, recv, at(z_, xy, zh))
            return carry

        lax.fori_loop(0, 7, one, 0)

        @pl.when(loops)
        def _():
            src, dst, send, recv = parts(i, z)[kind]
            pltpu.make_async_copy(src, dst, recv).start()

        @pl.when(jnp.logical_not(loops))
        def _():
            src, dst, send, recv = parts(i, z)[kind]
            push(src, dst, send, recv, at(z, xy, zh))

    def issue(n, carry):
        late = n - 6
        turn, third = late // 3, late % 3
        i = jnp.where(n < 6, n // 2, jnp.where(n < 12, jnp.where(third == 0, turn, turn + 3), n - 10))
        kind = jnp.where(n < 6, n % 2, jnp.where(jnp.logical_and(n < 12, third > 0), third - 1, 2))
        for option in range(3):

            @pl.when(kind == option)
            def _():
                spread(i, option)

        return carry

    def left_here(u):
        @pl.when(loops)
        def _():
            wait_for(kv.at[u, pl.ds(0, CHUNK - ROWS), :], kv_send.at[u])

        @pl.when(jnp.logical_not(loops))
        def _():
            wait_for(kv.at[u, pl.ds(0, CHUNK), :], kv_send.at[u])

    issue(0, 0)
    left_here(0)
    lax.fori_loop(1, FIRST, issue, 0)

    fetch.wait()
    lines[...] = jnp.zeros_like(lines)
    for h in range(2 * HEADS):
        row = (h // HEADS) * FLAG_ROWS + (h % HEADS) * 3
        lines[pl.ds(row, 3), pl.ds(0, COUNT)] = jnp.where(masks[h] == 1, 1.0, 0.0)
    shape = (2 * FLAG_ROWS, TILE)
    row = lax.broadcasted_iota(jnp.int32, shape, 0)
    third = (row % FLAG_ROWS) % 3
    head_ = (row // FLAG_ROWS) * HEADS + (row % FLAG_ROWS) // 3
    limit = jnp.full(shape, NEAR, jnp.int32)
    for h in range(2 * HEADS):
        limit = jnp.where(jnp.logical_and(head_ == h, type_ref[h] == 1), REACH, limit)
    allowed = jnp.zeros(shape, jnp.float32)
    pick_row = lax.broadcasted_iota(jnp.int32, (lines.shape[1], TILE), 0)
    pick_col = lax.broadcasted_iota(jnp.int32, (lines.shape[1], TILE), 1)
    col = lax.broadcasted_iota(jnp.int32, shape, 1)
    for t in range(3):
        shift = (ctx + t) % 2
        pick = (pick_row - pick_col == 3 * ctx + t - shift - REACH).astype(jnp.bfloat16)
        seen = jnp.dot(lines[...].astype(jnp.bfloat16), pick, preferred_element_type=jnp.float32)
        distance = jnp.abs(col - shift - REACH)
        seen = jnp.where(distance == 0, 1.0, jnp.where(distance <= limit, seen, 0.0))
        allowed = jnp.where(third == t, seen, allowed)
    for e in range(2):
        shown[e] = allowed[e * FLAG_ROWS : (e + 1) * FLAG_ROWS]

    for e in range(2):
        z_ = 2 * hd + e
        here = jnp.logical_and(loops, z_ == z)

        @pl.when(here)
        def _():
            pltpu.make_async_copy(shown.at[e], flags.at[core], flag_recv).start()

        @pl.when(jnp.logical_not(here))
        def _():
            push(shown.at[e], flags.at[core], flag_send.at[e], flag_recv, at(z_, xy, zh))

    def clear(slot, when):
        @pl.when(when)
        def _():
            def one(i, carry):
                kv[i, pl.ds(slot * CHUNK, CHUNK), :] = jnp.zeros((CHUNK, DIM), jnp.bfloat16)
                return carry

            lax.fori_loop(0, UNITS, one, 0)

    clear(0, chunk < 2)
    clear(1, chunk < 1)
    clear(3, chunk > CHUNKS - 2)
    clear(4, chunk > CHUNKS - 3)

    def slot(i, s):
        return kv.at[i, pl.ds(s * CHUNK, CHUNK), :]

    def send_own(i):
        wait_for(slot(i, 2), kv_recv.at[i])

        @pl.when(has_right)
        def _():
            push(slot(i, 2), slot(i, 1), y_send.at[0], near_recv.at[0, i], right)

        @pl.when(has_left)
        def _():
            push(slot(i, 2), slot(i, 3), y_send.at[1], near_recv.at[1, i], left)

    def both(*terms):
        out = terms[0]
        for term in terms[1:]:
            out = jnp.logical_and(out, term)
        return out

    def either(one, other):
        return jnp.logical_or(one, other)

    to_right = (both(inside, has_left), both(has_left, either(at_start, both(y == 1, first_row))))
    to_left = (both(inside, has_right), both(has_right, either(at_end, both(y == 2, last_row))))
    left_closes = both(at_end, has_left)
    right_closes = both(at_start, has_right)
    high_first = (y < 2, y % 2 == 0)
    has_low, has_high = chunk >= 2, chunk < CHUNKS - 2

    def pass_on(u, kind):
        @pl.when(has_left)
        def _():
            wait_for(slot(u, 1), near_recv.at[0, u])

        @pl.when(to_right[kind])
        def _():
            push(slot(u, 1), slot(u, 0), y_send.at[2 + kind], far_recv.at[0, u], right)

        if kind == 1:

            @pl.when(left_closes)
            def _():
                push(slot(u, 1), slot(u, 4), y_send.at[6], far_recv.at[1, u], closing)

        @pl.when(has_right)
        def _():
            wait_for(slot(u, 3), near_recv.at[1, u])

        @pl.when(to_left[kind])
        def _():
            push(slot(u, 3), slot(u, 4), y_send.at[4 + kind], far_recv.at[1, u], left)

        if kind == 1:

            @pl.when(right_closes)
            def _():
                push(slot(u, 3), slot(u, 0), y_send.at[7], far_recv.at[0, u], closing)

    def pass_across(u, kind):
        high = high_first[kind]

        @pl.when(both(high, has_high))
        def _():
            wait_for(slot(u, 4), far_recv.at[1, u])

        @pl.when(both(high, has_ahead))
        def _():
            push(slot(u, 4), slot(u, 0), y_send.at[8 + kind], far_recv.at[0, u], ahead)

        @pl.when(both(jnp.logical_not(high), has_low))
        def _():
            wait_for(slot(u, 0), far_recv.at[0, u])

        @pl.when(both(jnp.logical_not(high), has_back))
        def _():
            push(slot(u, 0), slot(u, 4), y_send.at[10 + kind], far_recv.at[1, u], back)

    def see():
        wait_for(flags, flag_recv)
        spots = lax.broadcasted_iota(jnp.int32, (TILE, KEYS), 1) // TILE
        rows_ = lax.broadcasted_iota(jnp.int32, (TILE, KEYS), 0)
        wide = (spots == rows_).astype(jnp.bfloat16)
        for c in range(2):
            seen = jnp.dot(flags[c].astype(jnp.bfloat16), wide, preferred_element_type=jnp.float32)
            seen = (seen - 1.0) * LOW
            for i in range(HEADS):
                bias[pl.ds(i * TILES + 3 * c, 3), :] = seen[3 * i : 3 * i + 3]

    def attend(i):
        def arrived(u, kind):
            @pl.when(both(high_first[kind], has_low))
            def _():
                wait_for(slot(u, 0), far_recv.at[0, u])

            @pl.when(both(jnp.logical_not(high_first[kind]), has_high))
            def _():
                wait_for(slot(u, 4), far_recv.at[1, u])

        wait_for(qb.at[i], q_recv.at[i])
        arrived(2 * i, 0)
        for p in range(CHUNK // PAIR):
            start = p * PAIR
            q = qb[i, pl.ds(start, PAIR), :]
            best = jnp.full((PAIR, TILE), -3e38, jnp.float32)
            for j in range(0, KEYS, STEP):
                keys = kv[2 * i, pl.ds(start + j, STEP), :]
                s = lax.dot_general(q, keys, (((1,), (1,)), ((), ())), preferred_element_type=jnp.float32)
                even = s[:TILE] + bias[pl.ds(i * TILES + 2 * p, 1), pl.ds(j, STEP)]
                odd = s[TILE:] + bias[pl.ds(i * TILES + 2 * p + 1, 1), pl.ds(j, STEP)]
                s = jnp.concatenate([even, odd], axis=0)
                held[p, :, pl.ds(j, STEP)] = s
                for t in range(0, STEP, TILE):
                    best = jnp.maximum(best, s[:, t : t + TILE])
            best = jnp.max(best, axis=1, keepdims=True)
            total = jnp.zeros((PAIR, TILE), jnp.float32)
            for j in range(0, KEYS, STEP):
                raw = jnp.exp2((held[p, :, pl.ds(j, STEP)] - best) * RATE)
                for t in range(0, STEP, TILE):
                    total = total + raw[:, t : t + TILE]
                weights[p, :, pl.ds(j, STEP)] = raw.astype(jnp.bfloat16)
            totals[p] = jnp.broadcast_to(jnp.sum(total, axis=1, keepdims=True), (PAIR, TILE))

        arrived(2 * i + 1, 1)
        for p in range(CHUNK // PAIR):
            start = p * PAIR
            values = kv[2 * i + 1, pl.ds(start, KEYS), :]
            mixed = jnp.dot(weights[p], values, preferred_element_type=jnp.float32)
            ob[i, pl.ds(start, PAIR), :] = (mixed / totals[p]).astype(jnp.bfloat16)

        cols = pl.ds(pl.multiple_of((z * HEADS + i) * DIM, DIM), DIM)

        def owner(n):
            zl = (hd + n // 2) % 4
            cs = (core + n) % 2
            return ob.at[i, pl.ds(pl.multiple_of(cs * 384 + zl * ROWS, 16), ROWS), :], at(core * 4 + zl, xy, cs)

        @pl.when(loops)
        def _():
            pltpu.make_async_copy(owner(0)[0], o_ref.at[:, cols], o_recv).start()

        @pl.when(jnp.logical_not(loops))
        def _():
            push(owner(0)[0], o_ref.at[:, cols], o_send, o_recv, owner(0)[1])

        def one(n, carry):
            src, to = owner(n)
            push(src, o_ref.at[:, cols], o_send, o_recv, to)
            return carry

        lax.fori_loop(1, 8, one, 0)

    def advance(s, carry):
        @pl.when(s < HEADS)
        def _():
            for t in range(2):
                u = 2 * s + t
                send_own(u)
                low = jnp.where(u == 0, FIRST, jnp.minimum(PIECES, LEAD + 2 * u - 2))
                lax.fori_loop(low, jnp.minimum(PIECES, LEAD + 2 * u), issue, 0)

                @pl.when(u > 0)
                def _():
                    pass_on(u - 1, 1 - t)

                @pl.when(u > 1)
                def _():
                    pass_across(u - 2, t)

            @pl.when(s == 0)
            def _():
                see()

        @pl.when(s == HEADS)
        def _():
            pass_on(UNITS - 1, 1)
            pass_across(UNITS - 2, 0)

        @pl.when(s == HEADS + 1)
        def _():
            pass_across(UNITS - 1, 1)

        @pl.when(s >= 2)
        def _():
            attend(s - 2)

        return carry

    lax.fori_loop(0, HEADS + 2, advance, 0)

    wait_for(o_ref, o_recv)

    def sent(rows):
        wait_for(qb.at[:, pl.ds(0, rows), :], q_send)
        wait_for(ob.at[:, pl.ds(0, rows), :], o_send)

    @pl.when(loops)
    def _():
        sent(CHUNK - ROWS)

    @pl.when(jnp.logical_not(loops))
    def _():
        sent(CHUNK)

    def drain(u, carry):
        left_here(u)
        return carry

    lax.fori_loop(1, UNITS, drain, 0)

    for e in range(2):

        @pl.when(jnp.logical_not(jnp.logical_and(loops, 2 * hd + e == z)))
        def _():
            wait_for(shown.at[e], flag_send.at[e])

    gone = [(has_right, 0, UNITS), (has_left, 1, UNITS), (left_closes, 6, HEADS), (right_closes, 7, HEADS)]
    for kind in range(2):
        gone += [(to_right[kind], 2 + kind, HEADS), (to_left[kind], 4 + kind, HEADS)]
        gone += [(both(high_first[kind], has_ahead), 8 + kind, HEADS)]
        gone += [(both(jnp.logical_not(high_first[kind]), has_back), 10 + kind, HEADS)]
    for there, which, units in gone:

        @pl.when(there)
        def _():
            wait_for(kv.at[pl.ds(0, units), pl.ds(0, CHUNK), :], y_send.at[which])


def per_device(query_rows, key_rows, value_rows, block_mask, head_type):
    any_ = pl.BlockSpec(memory_space=pltpu.HBM)
    dma = pltpu.SemaphoreType.DMA
    return pl.pallas_call(
        kernel,
        out_shape=jax.ShapeDtypeStruct(query_rows.shape, jnp.bfloat16),
        in_specs=[any_] * 4 + [pl.BlockSpec(memory_space=pltpu.SMEM)],
        out_specs=pl.BlockSpec(memory_space=pltpu.VMEM),
        scratch_shapes=[
            pltpu.VMEM((UNITS, WINDOW, DIM), jnp.bfloat16),
            pltpu.VMEM((HEADS, CHUNK, DIM), jnp.bfloat16),
            pltpu.VMEM((HEADS, CHUNK, DIM), jnp.bfloat16),
            pltpu.VMEM(block_mask.shape, jnp.int32),
            pltpu.VMEM((2 * FLAG_ROWS, 2 * TILE), jnp.float32),
            pltpu.VMEM((2, FLAG_ROWS, TILE), jnp.float32),
            pltpu.VMEM((2, FLAG_ROWS, TILE), jnp.float32),
            pltpu.VMEM((HEADS * TILES + 2, KEYS), jnp.float32),
            pltpu.VMEM((CHUNK // PAIR, PAIR, KEYS), jnp.float32),
            pltpu.VMEM((CHUNK // PAIR, PAIR, KEYS), jnp.bfloat16),
            pltpu.VMEM((CHUNK // PAIR, PAIR, TILE), jnp.float32),
            dma, dma((UNITS,)), dma, dma((2,)), dma, dma((12,)),
            dma((UNITS,)), dma((HEADS,)), dma, dma, dma((2, UNITS)), dma((2, UNITS)),
        ],
        compiler_params=pltpu.CompilerParams(
            collective_id=0, has_side_effects=True, vmem_limit_bytes=56 * 1024 * 1024
        ),
    )(query_rows, key_rows, value_rows, block_mask, head_type)


def solution(mesh):
    placed = (
        P(("ctx", "head"), None),
        P(("ctx", "head"), None),
        P(("ctx", "head"), None),
        P("head", "ctx", None),
        P("head"),
    )
    return jax.shard_map(
        per_device, mesh=mesh, in_specs=placed, out_specs=P(("ctx", "head"), None), check_vma=False
    )
```

```python
import math

import jax
import jax.numpy as jnp
from jax import lax
from jax.experimental import pallas as pl
from jax.experimental.pallas import tpu as pltpu
from jax.sharding import PartitionSpec as P

MESH = pl.DeviceIdType.MESH
TILE = 128
DIM = 128
HEADS = 5
ROWS = 96
CHUNK = 768
TILES = CHUNK // TILE
REACH = 12
NEAR = 3
PAIR = 2 * TILE
SPAN = 2 * REACH + 2
KEYS = SPAN * TILE
STEP = 256
UNITS = 2 * HEADS
PIECES = 3 * HEADS
FIRST = 2
LAG_ON, LAG_ACROSS = 1, 3
LAG_ATTEND, TURN = 2, 1
LEAD = 7
WINDOW = 5 * CHUNK
OWN = 2 * CHUNK
CHUNKS = 32
RING = 4
FLAG_ROWS = 16
COUNT = 192
LOW = 1e30
RATE = math.log2(math.e) / math.sqrt(DIM)


def wait_for(ref, sem):
    pltpu.make_async_copy(ref, ref, sem).wait()


def kernel(
    q_ref, k_ref, v_ref, mask_ref, type_ref, o_ref,
    kv, qb, ob, masks, lines, shown, flags, bias, held, weights, totals,
    mask_copy, kv_send, q_send, flag_send, o_send, y_send,
    kv_recv, q_recv, flag_recv, o_recv, near_recv, far_recv,
):
    hd = lax.axis_index("head")
    ctx = lax.axis_index("ctx")
    zh = ctx // 32
    xy = (ctx // 2) % 16
    core = ctx % 2
    z = zh * 4 + hd
    chunk = core * 16 + xy
    loops = zh == core
    has_left = chunk > 0
    has_right = chunk < CHUNKS - 1

    def at(z_, xy_, core_):
        return {"head": z_ % 4, "ctx": (z_ // 4) * 32 + xy_ * 2 + core_}

    def beside(by):
        other = (chunk + by + CHUNKS) % CHUNKS
        return at(z, other % 16, other // 16)

    left, right = beside(-1), beside(1)
    back, ahead = beside(-RING), beside(RING)
    y = xy % RING
    first_row = chunk < RING
    last_row = chunk >= CHUNKS - RING
    at_start, at_end = y == 0, y == RING - 1
    inside = jnp.logical_not(jnp.logical_or(at_start, at_end))
    closing = beside(jnp.where(at_start, RING - 1, 1 - RING))

    barrier = pltpu.get_barrier_semaphore()

    def greet(n, carry):
        other = (z * 2 + core + n) % 16
        pl.semaphore_signal(barrier, inc=1, device_id=at(other // 2, xy, other % 2), device_id_type=MESH)
        return carry

    lax.fori_loop(1, 16, greet, 0)

    has_back, has_ahead = jnp.logical_not(first_row), jnp.logical_not(last_row)
    has_closing = jnp.logical_not(inside)
    partners = ((has_left, left), (has_right, right), (has_back, back), (has_ahead, ahead), (has_closing, closing))
    for there, partner in partners:

        @pl.when(there)
        def _():
            pl.semaphore_signal(barrier, inc=1, device_id=partner, device_id_type=MESH)

    pl.semaphore_wait(barrier, 15 + sum(there.astype(jnp.int32) for there, _ in partners))

    mine = core * 384 + hd * ROWS

    fetch = pltpu.make_async_copy(mask_ref, masks, mask_copy)
    fetch.start()

    def parts(i, z_):
        cols = pl.ds(pl.multiple_of((z_ * HEADS + i) * DIM, DIM), DIM)
        rows = pl.ds(pl.multiple_of(OWN + mine, 16), ROWS)
        q_rows = pl.ds(pl.multiple_of(mine, 16), ROWS)
        return (
            (k_ref.at[:, cols], kv.at[2 * i, rows, :], kv_send.at[2 * i], kv_recv.at[2 * i]),
            (v_ref.at[:, cols], kv.at[2 * i + 1, rows, :], kv_send.at[2 * i + 1], kv_recv.at[2 * i + 1]),
            (q_ref.at[:, cols], qb.at[i, q_rows, :], q_send, q_recv.at[i]),
        )

    def push(src, dst, send, recv, to):
        pltpu.make_async_remote_copy(
            src_ref=src, dst_ref=dst, send_sem=send, recv_sem=recv, device_id=to, device_id_type=MESH
        ).start()

    def spread(i, kind):
        def one(j, carry):
            half = j // 2 + 1
            step = jnp.where(j % 2 == 0, half, 8 - half)
            z_ = (z + step) % 8
            src, dst, send, recv = parts(i, z_)[kind]
            push(src, dst, send, recv, at(z_, xy, zh))
            return carry

        lax.fori_loop(0, 7, one, 0)

        @pl.when(loops)
        def _():
            src, dst, send, recv = parts(i, z)[kind]
            pltpu.make_async_copy(src, dst, recv).start()

        @pl.when(jnp.logical_not(loops))
        def _():
            src, dst, send, recv = parts(i, z)[kind]
            push(src, dst, send, recv, at(z, xy, zh))

    def issue(n, carry):
        late = n - 6
        turn, third = late // 3, late % 3
        i = jnp.where(n < 6, n // 2, jnp.where(n < 12, jnp.where(third == 0, turn, turn + 3), n - 10))
        kind = jnp.where(n < 6, n % 2, jnp.where(jnp.logical_and(n < 12, third > 0), third - 1, 2))
        for option in range(3):

            @pl.when(kind == option)
            def _():
                spread(i, option)

        return carry

    def left_here(u):
        @pl.when(loops)
        def _():
            wait_for(kv.at[u, pl.ds(0, CHUNK - ROWS), :], kv_send.at[u])

        @pl.when(jnp.logical_not(loops))
        def _():
            wait_for(kv.at[u, pl.ds(0, CHUNK), :], kv_send.at[u])

    issue(0, 0)
    left_here(0)
    lax.fori_loop(1, FIRST, issue, 0)

    fetch.wait()
    lines[...] = jnp.zeros_like(lines)
    for h in range(2 * HEADS):
        row = (h // HEADS) * FLAG_ROWS + (h % HEADS) * 3
        lines[pl.ds(row, 3), pl.ds(0, COUNT)] = jnp.where(masks[h] == 1, 1.0, 0.0)
    shape = (2 * FLAG_ROWS, TILE)
    row = lax.broadcasted_iota(jnp.int32, shape, 0)
    third = (row % FLAG_ROWS) % 3
    head_ = (row // FLAG_ROWS) * HEADS + (row % FLAG_ROWS) // 3
    limit = jnp.full(shape, NEAR, jnp.int32)
    for h in range(2 * HEADS):
        limit = jnp.where(jnp.logical_and(head_ == h, type_ref[h] == 1), REACH, limit)
    allowed = jnp.zeros(shape, jnp.float32)
    pick_row = lax.broadcasted_iota(jnp.int32, (lines.shape[1], TILE), 0)
    pick_col = lax.broadcasted_iota(jnp.int32, (lines.shape[1], TILE), 1)
    col = lax.broadcasted_iota(jnp.int32, shape, 1)
    for t in range(3):
        shift = (ctx + t) % 2
        pick = (pick_row - pick_col == 3 * ctx + t - shift - REACH).astype(jnp.bfloat16)
        seen = jnp.dot(lines[...].astype(jnp.bfloat16), pick, preferred_element_type=jnp.float32)
        distance = jnp.abs(col - shift - REACH)
        seen = jnp.where(distance == 0, 1.0, jnp.where(distance <= limit, seen, 0.0))
        allowed = jnp.where(third == t, seen, allowed)
    for e in range(2):
        shown[e] = allowed[e * FLAG_ROWS : (e + 1) * FLAG_ROWS]

    for e in range(2):
        z_ = 2 * hd + e
        here = jnp.logical_and(loops, z_ == z)

        @pl.when(here)
        def _():
            pltpu.make_async_copy(shown.at[e], flags.at[core], flag_recv).start()

        @pl.when(jnp.logical_not(here))
        def _():
            push(shown.at[e], flags.at[core], flag_send.at[e], flag_recv, at(z_, xy, zh))

    def clear(slot, when):
        @pl.when(when)
        def _():
            def one(i, carry):
                kv[i, pl.ds(slot * CHUNK, CHUNK), :] = jnp.zeros((CHUNK, DIM), jnp.bfloat16)
                return carry

            lax.fori_loop(0, UNITS, one, 0)

    clear(0, chunk < 2)
    clear(1, chunk < 1)
    clear(3, chunk > CHUNKS - 2)
    clear(4, chunk > CHUNKS - 3)

    def slot(i, s):
        return kv.at[i, pl.ds(s * CHUNK, CHUNK), :]

    def send_own(i):
        wait_for(slot(i, 2), kv_recv.at[i])

        @pl.when(has_right)
        def _():
            push(slot(i, 2), slot(i, 1), y_send.at[0], near_recv.at[0, i], right)

        @pl.when(has_left)
        def _():
            push(slot(i, 2), slot(i, 3), y_send.at[1], near_recv.at[1, i], left)

    def both(*terms):
        out = terms[0]
        for term in terms[1:]:
            out = jnp.logical_and(out, term)
        return out

    def either(one, other):
        return jnp.logical_or(one, other)

    to_right = (both(inside, has_left), both(has_left, either(at_start, both(y == 1, first_row))))
    to_left = (both(inside, has_right), both(has_right, either(at_end, both(y == 2, last_row))))
    left_closes = both(at_end, has_left)
    right_closes = both(at_start, has_right)
    high_first = (y < 2, y % 2 == 0)
    has_low, has_high = chunk >= 2, chunk < CHUNKS - 2

    def pass_on(u, kind):
        @pl.when(has_left)
        def _():
            wait_for(slot(u, 1), near_recv.at[0, u])

        @pl.when(to_right[kind])
        def _():
            push(slot(u, 1), slot(u, 0), y_send.at[2 + kind], far_recv.at[0, u], right)

        if kind == 1:

            @pl.when(left_closes)
            def _():
                push(slot(u, 1), slot(u, 4), y_send.at[6], far_recv.at[1, u], closing)

        @pl.when(has_right)
        def _():
            wait_for(slot(u, 3), near_recv.at[1, u])

        @pl.when(to_left[kind])
        def _():
            push(slot(u, 3), slot(u, 4), y_send.at[4 + kind], far_recv.at[1, u], left)

        if kind == 1:

            @pl.when(right_closes)
            def _():
                push(slot(u, 3), slot(u, 0), y_send.at[7], far_recv.at[0, u], closing)

    def pass_across(u, kind):
        high = high_first[kind]

        @pl.when(both(high, has_high))
        def _():
            wait_for(slot(u, 4), far_recv.at[1, u])

        @pl.when(both(high, has_ahead))
        def _():
            push(slot(u, 4), slot(u, 0), y_send.at[8 + kind], far_recv.at[0, u], ahead)

        @pl.when(both(jnp.logical_not(high), has_low))
        def _():
            wait_for(slot(u, 0), far_recv.at[0, u])

        @pl.when(both(jnp.logical_not(high), has_back))
        def _():
            push(slot(u, 0), slot(u, 4), y_send.at[10 + kind], far_recv.at[1, u], back)

    def see():
        wait_for(flags, flag_recv)
        spots = lax.broadcasted_iota(jnp.int32, (TILE, KEYS), 1) // TILE
        rows_ = lax.broadcasted_iota(jnp.int32, (TILE, KEYS), 0)
        wide = (spots == rows_).astype(jnp.bfloat16)
        for c in range(2):
            seen = jnp.dot(flags[c].astype(jnp.bfloat16), wide, preferred_element_type=jnp.float32)
            seen = (seen - 1.0) * LOW
            for i in range(HEADS):
                bias[pl.ds(i * TILES + 3 * c, 3), :] = seen[3 * i : 3 * i + 3]

    def attend(i):
        def arrived(u, kind):
            @pl.when(both(high_first[kind], has_low))
            def _():
                wait_for(slot(u, 0), far_recv.at[0, u])

            @pl.when(both(jnp.logical_not(high_first[kind]), has_high))
            def _():
                wait_for(slot(u, 4), far_recv.at[1, u])

        wait_for(qb.at[i], q_recv.at[i])
        arrived(2 * i, 0)
        for p in range(CHUNK // PAIR):
            start = p * PAIR
            q = qb[i, pl.ds(start, PAIR), :]
            best = jnp.full((PAIR, TILE), -3e38, jnp.float32)
            for j in range(0, KEYS, STEP):
                keys = kv[2 * i, pl.ds(start + j, STEP), :]
                s = lax.dot_general(q, keys, (((1,), (1,)), ((), ())), preferred_element_type=jnp.float32)
                even = s[:TILE] + bias[pl.ds(i * TILES + 2 * p, 1), pl.ds(j, STEP)]
                odd = s[TILE:] + bias[pl.ds(i * TILES + 2 * p + 1, 1), pl.ds(j, STEP)]
                s = jnp.concatenate([even, odd], axis=0)
                held[p, :, pl.ds(j, STEP)] = s
                for t in range(0, STEP, TILE):
                    best = jnp.maximum(best, s[:, t : t + TILE])
            best = jnp.max(best, axis=1, keepdims=True)
            total = jnp.zeros((PAIR, TILE), jnp.float32)
            for j in range(0, KEYS, STEP):
                raw = jnp.exp2((held[p, :, pl.ds(j, STEP)] - best) * RATE)
                for t in range(0, STEP, TILE):
                    total = total + raw[:, t : t + TILE]
                weights[p, :, pl.ds(j, STEP)] = raw.astype(jnp.bfloat16)
            totals[p] = jnp.broadcast_to(jnp.sum(total, axis=1, keepdims=True), (PAIR, TILE))

        arrived(2 * i + 1, 1)
        for p in range(CHUNK // PAIR):
            start = p * PAIR
            values = kv[2 * i + 1, pl.ds(start, KEYS), :]
            mixed = jnp.dot(weights[p], values, preferred_element_type=jnp.float32)
            ob[i, pl.ds(start, PAIR), :] = (mixed / totals[p]).astype(jnp.bfloat16)

        cols = pl.ds(pl.multiple_of((z * HEADS + i) * DIM, DIM), DIM)

        def owner(n):
            zl = (hd + n // 2) % 4
            cs = (core + n) % 2
            return ob.at[i, pl.ds(pl.multiple_of(cs * 384 + zl * ROWS, 16), ROWS), :], at(core * 4 + zl, xy, cs)

        @pl.when(loops)
        def _():
            pltpu.make_async_copy(owner(0)[0], o_ref.at[:, cols], o_recv).start()

        @pl.when(jnp.logical_not(loops))
        def _():
            push(owner(0)[0], o_ref.at[:, cols], o_send, o_recv, owner(0)[1])

        def one(n, carry):
            src, to = owner(n)
            push(src, o_ref.at[:, cols], o_send, o_recv, to)
            return carry

        lax.fori_loop(1, 8, one, 0)

    def within(n, count):
        return jnp.logical_and(n >= 0, n < count)

    def advance(s, carry):
        for t in range(2):
            u = 2 * s + t

            @pl.when(u < UNITS)
            def _():
                send_own(u)
                low = jnp.where(u == 0, FIRST, jnp.minimum(PIECES, LEAD + 2 * u - 2))
                lax.fori_loop(low, jnp.minimum(PIECES, LEAD + 2 * u), issue, 0)

            @pl.when(within(u - LAG_ON, UNITS))
            def _():
                pass_on(u - LAG_ON, (t - LAG_ON) % 2)

            @pl.when(within(u - LAG_ACROSS, UNITS))
            def _():
                pass_across(u - LAG_ACROSS, (t - LAG_ACROSS) % 2)

            if t == TURN:

                @pl.when(s == 0)
                def _():
                    see()

                @pl.when(within(s - LAG_ATTEND, HEADS))
                def _():
                    attend(s - LAG_ATTEND)

        return carry

    lax.fori_loop(0, HEADS + LAG_ATTEND, advance, 0)

    wait_for(o_ref, o_recv)

    def sent(rows):
        wait_for(qb.at[:, pl.ds(0, rows), :], q_send)
        wait_for(ob.at[:, pl.ds(0, rows), :], o_send)

    @pl.when(loops)
    def _():
        sent(CHUNK - ROWS)

    @pl.when(jnp.logical_not(loops))
    def _():
        sent(CHUNK)

    def drain(u, carry):
        left_here(u)
        return carry

    lax.fori_loop(1, UNITS, drain, 0)

    for e in range(2):

        @pl.when(jnp.logical_not(jnp.logical_and(loops, 2 * hd + e == z)))
        def _():
            wait_for(shown.at[e], flag_send.at[e])

    gone = [(has_right, 0, UNITS), (has_left, 1, UNITS), (left_closes, 6, HEADS), (right_closes, 7, HEADS)]
    for kind in range(2):
        gone += [(to_right[kind], 2 + kind, HEADS), (to_left[kind], 4 + kind, HEADS)]
        gone += [(both(high_first[kind], has_ahead), 8 + kind, HEADS)]
        gone += [(both(jnp.logical_not(high_first[kind]), has_back), 10 + kind, HEADS)]
    for there, which, units in gone:

        @pl.when(there)
        def _():
            wait_for(kv.at[pl.ds(0, units), pl.ds(0, CHUNK), :], y_send.at[which])


def per_device(query_rows, key_rows, value_rows, block_mask, head_type):
    any_ = pl.BlockSpec(memory_space=pltpu.HBM)
    dma = pltpu.SemaphoreType.DMA
    return pl.pallas_call(
        kernel,
        out_shape=pltpu.VMEM(query_rows.shape, jnp.bfloat16),
        in_specs=[any_] * 4 + [pl.BlockSpec(memory_space=pltpu.SMEM)],
        out_specs=pl.BlockSpec(memory_space=pl.ANY),
        scratch_shapes=[
            pltpu.VMEM((UNITS, WINDOW, DIM), jnp.bfloat16),
            pltpu.VMEM((HEADS, CHUNK, DIM), jnp.bfloat16),
            pltpu.VMEM((HEADS, CHUNK, DIM), jnp.bfloat16),
            pltpu.VMEM(block_mask.shape, jnp.int32),
            pltpu.VMEM((2 * FLAG_ROWS, 2 * TILE), jnp.float32),
            pltpu.VMEM((2, FLAG_ROWS, TILE), jnp.float32),
            pltpu.VMEM((2, FLAG_ROWS, TILE), jnp.float32),
            pltpu.VMEM((HEADS * TILES + 2, KEYS), jnp.float32),
            pltpu.VMEM((CHUNK // PAIR, PAIR, KEYS), jnp.float32),
            pltpu.VMEM((CHUNK // PAIR, PAIR, KEYS), jnp.bfloat16),
            pltpu.VMEM((CHUNK // PAIR, PAIR, TILE), jnp.float32),
            dma, dma((UNITS,)), dma, dma((2,)), dma, dma((12,)),
            dma((UNITS,)), dma((HEADS,)), dma, dma, dma((2, UNITS)), dma((2, UNITS)),
        ],
        compiler_params=pltpu.CompilerParams(
            collective_id=0, has_side_effects=True, vmem_limit_bytes=56 * 1024 * 1024
        ),
    )(query_rows, key_rows, value_rows, block_mask, head_type)


def solution(mesh):
    placed = (
        P(("ctx", "head"), None),
        P(("ctx", "head"), None),
        P(("ctx", "head"), None),
        P("head", "ctx", None),
        P("head"),
    )
    return jax.shard_map(
        per_device, mesh=mesh, in_specs=placed, out_specs=P(("ctx", "head"), None), check_vma=False
    )
```

```python
import math

import jax
import jax.numpy as jnp
from jax import lax
from jax.experimental import pallas as pl
from jax.experimental.pallas import tpu as pltpu
from jax.sharding import PartitionSpec as P

MESH = pl.DeviceIdType.MESH
TILE = 128
DIM = 128
HEADS = 5
ROWS = 96
CHUNK = 768
TILES = CHUNK // TILE
REACH = 12
NEAR = 3
PAIR = 2 * TILE
SPAN = 2 * REACH + 2
KEYS = SPAN * TILE
STEP = 256
UNITS = 2 * HEADS
PIECES = 3 * HEADS
FIRST = 2
LAG_ON, LAG_ACROSS = 1, 3
START, LATE = 5, 13
AHEAD = 4
WINDOW = 5 * CHUNK
OWN = 2 * CHUNK
CHUNKS = 32
RING = 4
FLAG_ROWS = 16
COUNT = 192
LOW = 1e30
RATE = math.log2(math.e) / math.sqrt(DIM)


def wait_for(ref, sem):
    pltpu.make_async_copy(ref, ref, sem).wait()


def kernel(
    q_ref, k_ref, v_ref, mask_ref, type_ref, o_ref,
    kv, qb, ob, masks, lines, shown, flags, bias, held, weights, totals,
    mask_copy, kv_send, q_send, flag_send, o_send, y_send,
    kv_recv, q_recv, flag_recv, o_recv, near_recv, far_recv,
):
    hd = lax.axis_index("head")
    ctx = lax.axis_index("ctx")
    zh = ctx // 32
    xy = (ctx // 2) % 16
    core = ctx % 2
    z = zh * 4 + hd
    chunk = core * 16 + xy
    loops = zh == core
    has_left = chunk > 0
    has_right = chunk < CHUNKS - 1

    def at(z_, xy_, core_):
        return {"head": z_ % 4, "ctx": (z_ // 4) * 32 + xy_ * 2 + core_}

    def beside(by):
        other = (chunk + by + CHUNKS) % CHUNKS
        return at(z, other % 16, other // 16)

    left, right = beside(-1), beside(1)
    back, ahead = beside(-RING), beside(RING)
    y = xy % RING
    first_row = chunk < RING
    last_row = chunk >= CHUNKS - RING
    at_start, at_end = y == 0, y == RING - 1
    inside = jnp.logical_not(jnp.logical_or(at_start, at_end))
    closing = beside(jnp.where(at_start, RING - 1, 1 - RING))

    barrier = pltpu.get_barrier_semaphore()

    def greet(n, carry):
        other = (z * 2 + core + n) % 16
        pl.semaphore_signal(barrier, inc=1, device_id=at(other // 2, xy, other % 2), device_id_type=MESH)
        return carry

    lax.fori_loop(1, 16, greet, 0)

    has_back, has_ahead = jnp.logical_not(first_row), jnp.logical_not(last_row)
    has_closing = jnp.logical_not(inside)
    partners = ((has_left, left), (has_right, right), (has_back, back), (has_ahead, ahead), (has_closing, closing))
    for there, partner in partners:

        @pl.when(there)
        def _():
            pl.semaphore_signal(barrier, inc=1, device_id=partner, device_id_type=MESH)

    pl.semaphore_wait(barrier, 15 + sum(there.astype(jnp.int32) for there, _ in partners))

    mine = core * 384 + hd * ROWS

    fetch = pltpu.make_async_copy(mask_ref, masks, mask_copy)
    fetch.start()

    def parts(i, z_):
        cols = pl.ds(pl.multiple_of((z_ * HEADS + i) * DIM, DIM), DIM)
        rows = pl.ds(pl.multiple_of(OWN + mine, 16), ROWS)
        q_rows = pl.ds(pl.multiple_of(mine, 16), ROWS)
        return (
            (k_ref.at[:, cols], kv.at[2 * i, rows, :], kv_send.at[2 * i], kv_recv.at[2 * i]),
            (v_ref.at[:, cols], kv.at[2 * i + 1, rows, :], kv_send.at[2 * i + 1], kv_recv.at[2 * i + 1]),
            (q_ref.at[:, cols], qb.at[i, q_rows, :], q_send, q_recv.at[i]),
        )

    def push(src, dst, send, recv, to):
        pltpu.make_async_remote_copy(
            src_ref=src, dst_ref=dst, send_sem=send, recv_sem=recv, device_id=to, device_id_type=MESH
        ).start()

    def spread(i, kind):
        def one(j, carry):
            half = j // 2 + 1
            step = jnp.where(j % 2 == 0, half, 8 - half)
            z_ = (z + step) % 8
            src, dst, send, recv = parts(i, z_)[kind]
            push(src, dst, send, recv, at(z_, xy, zh))
            return carry

        lax.fori_loop(0, 7, one, 0)

        @pl.when(loops)
        def _():
            src, dst, send, recv = parts(i, z)[kind]
            pltpu.make_async_copy(src, dst, recv).start()

        @pl.when(jnp.logical_not(loops))
        def _():
            src, dst, send, recv = parts(i, z)[kind]
            push(src, dst, send, recv, at(z, xy, zh))

    def issue(n, carry):
        late = n - 6
        turn, third = late // 3, late % 3
        i = jnp.where(n < 6, n // 2, jnp.where(n < 12, jnp.where(third == 0, turn, turn + 3), n - 10))
        kind = jnp.where(n < 6, n % 2, jnp.where(jnp.logical_and(n < 12, third > 0), third - 1, 2))
        for option in range(3):

            @pl.when(kind == option)
            def _():
                spread(i, option)

        return carry

    def left_here(u):
        @pl.when(loops)
        def _():
            wait_for(kv.at[u, pl.ds(0, CHUNK - ROWS), :], kv_send.at[u])

        @pl.when(jnp.logical_not(loops))
        def _():
            wait_for(kv.at[u, pl.ds(0, CHUNK), :], kv_send.at[u])

    issue(0, 0)

    fetch.wait()
    lines[...] = jnp.zeros_like(lines)
    for h in range(2 * HEADS):
        row = (h // HEADS) * FLAG_ROWS + (h % HEADS) * 3
        lines[pl.ds(row, 3), pl.ds(0, COUNT)] = jnp.where(masks[h] == 1, 1.0, 0.0)
    shape = (2 * FLAG_ROWS, TILE)
    row = lax.broadcasted_iota(jnp.int32, shape, 0)
    third = (row % FLAG_ROWS) % 3
    head_ = (row // FLAG_ROWS) * HEADS + (row % FLAG_ROWS) // 3
    limit = jnp.full(shape, NEAR, jnp.int32)
    for h in range(2 * HEADS):
        limit = jnp.where(jnp.logical_and(head_ == h, type_ref[h] == 1), REACH, limit)
    allowed = jnp.zeros(shape, jnp.float32)
    pick_row = lax.broadcasted_iota(jnp.int32, (lines.shape[1], TILE), 0)
    pick_col = lax.broadcasted_iota(jnp.int32, (lines.shape[1], TILE), 1)
    col = lax.broadcasted_iota(jnp.int32, shape, 1)
    for t in range(3):
        shift = (ctx + t) % 2
        pick = (pick_row - pick_col == 3 * ctx + t - shift - REACH).astype(jnp.bfloat16)
        seen = jnp.dot(lines[...].astype(jnp.bfloat16), pick, preferred_element_type=jnp.float32)
        distance = jnp.abs(col - shift - REACH)
        seen = jnp.where(distance == 0, 1.0, jnp.where(distance <= limit, seen, 0.0))
        allowed = jnp.where(third == t, seen, allowed)
    for e in range(2):
        shown[e] = allowed[e * FLAG_ROWS : (e + 1) * FLAG_ROWS]

    for e in range(2):
        z_ = 2 * hd + e
        here = jnp.logical_and(loops, z_ == z)

        @pl.when(here)
        def _():
            pltpu.make_async_copy(shown.at[e], flags.at[core], flag_recv).start()

        @pl.when(jnp.logical_not(here))
        def _():
            push(shown.at[e], flags.at[core], flag_send.at[e], flag_recv, at(z_, xy, zh))

    left_here(0)
    lax.fori_loop(1, FIRST, issue, 0)

    def clear(slot, when):
        @pl.when(when)
        def _():
            def one(i, carry):
                kv[i, pl.ds(slot * CHUNK, CHUNK), :] = jnp.zeros((CHUNK, DIM), jnp.bfloat16)
                return carry

            lax.fori_loop(0, UNITS, one, 0)

    clear(0, chunk < 2)
    clear(1, chunk < 1)
    clear(3, chunk > CHUNKS - 2)
    clear(4, chunk > CHUNKS - 3)

    def slot(i, s):
        return kv.at[i, pl.ds(s * CHUNK, CHUNK), :]

    def send_own(i):
        wait_for(slot(i, 2), kv_recv.at[i])

        @pl.when(has_right)
        def _():
            push(slot(i, 2), slot(i, 1), y_send.at[0], near_recv.at[0, i], right)

        @pl.when(has_left)
        def _():
            push(slot(i, 2), slot(i, 3), y_send.at[1], near_recv.at[1, i], left)

    def both(*terms):
        out = terms[0]
        for term in terms[1:]:
            out = jnp.logical_and(out, term)
        return out

    def either(one, other):
        return jnp.logical_or(one, other)

    def way(kind, keys, values):
        return either(both(kind == 0, keys), both(kind == 1, values))

    to_right = (both(inside, has_left), both(has_left, either(at_start, both(y == 1, first_row))))
    to_left = (both(inside, has_right), both(has_right, either(at_end, both(y == 2, last_row))))
    left_closes = both(at_end, has_left)
    right_closes = both(at_start, has_right)
    high_first = (y < 2, y % 2 == 0)
    has_low, has_high = chunk >= 2, chunk < CHUNKS - 2

    def pass_on(u, kind):
        @pl.when(has_left)
        def _():
            wait_for(slot(u, 1), near_recv.at[0, u])

        @pl.when(way(kind, *to_right))
        def _():
            push(slot(u, 1), slot(u, 0), y_send.at[2 + kind], far_recv.at[0, u], right)

        @pl.when(both(kind == 1, left_closes))
        def _():
            push(slot(u, 1), slot(u, 4), y_send.at[6], far_recv.at[1, u], closing)

        @pl.when(has_right)
        def _():
            wait_for(slot(u, 3), near_recv.at[1, u])

        @pl.when(way(kind, *to_left))
        def _():
            push(slot(u, 3), slot(u, 4), y_send.at[4 + kind], far_recv.at[1, u], left)

        @pl.when(both(kind == 1, right_closes))
        def _():
            push(slot(u, 3), slot(u, 0), y_send.at[7], far_recv.at[0, u], closing)

    def pass_across(u, kind):
        high = way(kind, *high_first)

        @pl.when(both(high, has_high))
        def _():
            wait_for(slot(u, 4), far_recv.at[1, u])

        @pl.when(both(high, has_ahead))
        def _():
            push(slot(u, 4), slot(u, 0), y_send.at[8 + kind], far_recv.at[0, u], ahead)

        @pl.when(both(jnp.logical_not(high), has_low))
        def _():
            wait_for(slot(u, 0), far_recv.at[0, u])

        @pl.when(both(jnp.logical_not(high), has_back))
        def _():
            push(slot(u, 0), slot(u, 4), y_send.at[10 + kind], far_recv.at[1, u], back)

    def see():
        wait_for(flags, flag_recv)
        spots = lax.broadcasted_iota(jnp.int32, (TILE, KEYS), 1) // TILE
        rows_ = lax.broadcasted_iota(jnp.int32, (TILE, KEYS), 0)
        wide = (spots == rows_).astype(jnp.bfloat16)
        for c in range(2):
            seen = jnp.dot(flags[c].astype(jnp.bfloat16), wide, preferred_element_type=jnp.float32)
            seen = (seen - 1.0) * LOW
            for i in range(HEADS):
                bias[pl.ds(i * TILES + 3 * c, 3), :] = seen[3 * i : 3 * i + 3]

    def attend(i):
        def arrived(u, kind):
            @pl.when(both(high_first[kind], has_low))
            def _():
                wait_for(slot(u, 0), far_recv.at[0, u])

            @pl.when(both(jnp.logical_not(high_first[kind]), has_high))
            def _():
                wait_for(slot(u, 4), far_recv.at[1, u])

        wait_for(qb.at[i], q_recv.at[i])
        arrived(2 * i, 0)
        for p in range(CHUNK // PAIR):
            start = p * PAIR
            q = qb[i, pl.ds(start, PAIR), :]
            best = jnp.full((PAIR, TILE), -3e38, jnp.float32)
            for j in range(0, KEYS, STEP):
                keys = kv[2 * i, pl.ds(start + j, STEP), :]
                s = lax.dot_general(q, keys, (((1,), (1,)), ((), ())), preferred_element_type=jnp.float32)
                even = s[:TILE] + bias[pl.ds(i * TILES + 2 * p, 1), pl.ds(j, STEP)]
                odd = s[TILE:] + bias[pl.ds(i * TILES + 2 * p + 1, 1), pl.ds(j, STEP)]
                s = jnp.concatenate([even, odd], axis=0)
                held[p, :, pl.ds(j, STEP)] = s
                for t in range(0, STEP, TILE):
                    best = jnp.maximum(best, s[:, t : t + TILE])
            best = jnp.max(best, axis=1, keepdims=True)
            total = jnp.zeros((PAIR, TILE), jnp.float32)
            for j in range(0, KEYS, STEP):
                raw = jnp.exp2((held[p, :, pl.ds(j, STEP)] - best) * RATE)
                for t in range(0, STEP, TILE):
                    total = total + raw[:, t : t + TILE]
                weights[p, :, pl.ds(j, STEP)] = raw.astype(jnp.bfloat16)
            totals[p] = jnp.broadcast_to(jnp.sum(total, axis=1, keepdims=True), (PAIR, TILE))

        arrived(2 * i + 1, 1)
        for p in range(CHUNK // PAIR):
            start = p * PAIR
            values = kv[2 * i + 1, pl.ds(start, KEYS), :]
            mixed = jnp.dot(weights[p], values, preferred_element_type=jnp.float32)
            ob[i, pl.ds(start, PAIR), :] = (mixed / totals[p]).astype(jnp.bfloat16)

        cols = pl.ds(pl.multiple_of((z * HEADS + i) * DIM, DIM), DIM)

        def owner(n):
            zl = (hd + n // 2) % 4
            cs = (core + n) % 2
            return ob.at[i, pl.ds(pl.multiple_of(cs * 384 + zl * ROWS, 16), ROWS), :], at(core * 4 + zl, xy, cs)

        @pl.when(loops)
        def _():
            pltpu.make_async_copy(owner(0)[0], o_ref.at[:, cols], o_recv).start()

        @pl.when(jnp.logical_not(loops))
        def _():
            push(owner(0)[0], o_ref.at[:, cols], o_send, o_recv, owner(0)[1])

        def one(n, carry):
            src, to = owner(n)
            push(src, o_ref.at[:, cols], o_send, o_recv, to)
            return carry

        lax.fori_loop(1, 8, one, 0)

    def place(u):
        return u + jnp.where(u >= 6, 1, 0) + jnp.where(u >= 8, 1, 0)

    def within(n, count):
        return jnp.logical_and(n >= 0, n < count)

    def advance(u, carry):
        @pl.when(u < UNITS)
        def _():
            send_own(u)
            low = jnp.where(u == 0, FIRST, jnp.minimum(PIECES, place(u - 1) + AHEAD))
            high = jnp.where(u == UNITS - 1, PIECES, jnp.minimum(PIECES, place(u) + AHEAD))
            lax.fori_loop(low, high, issue, 0)

        @pl.when(within(u - LAG_ON, UNITS))
        def _():
            pass_on(u - LAG_ON, (u - LAG_ON) % 2)

        @pl.when(within(u - LAG_ACROSS, UNITS))
        def _():
            pass_across(u - LAG_ACROSS, (u - LAG_ACROSS) % 2)

        @pl.when(u == 1)
        def _():
            see()

        @pl.when(jnp.logical_and(u >= START, either(u >= LATE, (u - START) % 2 == 0)))
        def _():
            attend(jnp.where(u >= LATE, u - LATE + (LATE - START + 1) // 2, (u - START) // 2))

        return carry

    lax.fori_loop(0, LATE + HEADS - (LATE - START + 1) // 2, advance, 0)

    wait_for(o_ref, o_recv)

    def sent(rows):
        wait_for(qb.at[:, pl.ds(0, rows), :], q_send)
        wait_for(ob.at[:, pl.ds(0, rows), :], o_send)

    @pl.when(loops)
    def _():
        sent(CHUNK - ROWS)

    @pl.when(jnp.logical_not(loops))
    def _():
        sent(CHUNK)

    def drain(u, carry):
        left_here(u)
        return carry

    lax.fori_loop(1, UNITS, drain, 0)

    for e in range(2):

        @pl.when(jnp.logical_not(jnp.logical_and(loops, 2 * hd + e == z)))
        def _():
            wait_for(shown.at[e], flag_send.at[e])

    gone = [(has_right, 0, UNITS), (has_left, 1, UNITS), (left_closes, 6, HEADS), (right_closes, 7, HEADS)]
    for kind in range(2):
        gone += [(to_right[kind], 2 + kind, HEADS), (to_left[kind], 4 + kind, HEADS)]
        gone += [(both(high_first[kind], has_ahead), 8 + kind, HEADS)]
        gone += [(both(jnp.logical_not(high_first[kind]), has_back), 10 + kind, HEADS)]
    for there, which, units in gone:

        @pl.when(there)
        def _():
            wait_for(kv.at[pl.ds(0, units), pl.ds(0, CHUNK), :], y_send.at[which])


def per_device(query_rows, key_rows, value_rows, block_mask, head_type):
    any_ = pl.BlockSpec(memory_space=pltpu.HBM)
    dma = pltpu.SemaphoreType.DMA
    return pl.pallas_call(
        kernel,
        out_shape=pltpu.VMEM(query_rows.shape, jnp.bfloat16),
        in_specs=[any_] * 4 + [pl.BlockSpec(memory_space=pltpu.SMEM)],
        out_specs=pl.BlockSpec(memory_space=pl.ANY),
        scratch_shapes=[
            pltpu.VMEM((UNITS, WINDOW, DIM), jnp.bfloat16),
            pltpu.VMEM((HEADS, CHUNK, DIM), jnp.bfloat16),
            pltpu.VMEM((HEADS, CHUNK, DIM), jnp.bfloat16),
            pltpu.VMEM(block_mask.shape, jnp.int32),
            pltpu.VMEM((2 * FLAG_ROWS, 2 * TILE), jnp.float32),
            pltpu.VMEM((2, FLAG_ROWS, TILE), jnp.float32),
            pltpu.VMEM((2, FLAG_ROWS, TILE), jnp.float32),
            pltpu.VMEM((HEADS * TILES + 2, KEYS), jnp.float32),
            pltpu.VMEM((CHUNK // PAIR, PAIR, KEYS), jnp.float32),
            pltpu.VMEM((CHUNK // PAIR, PAIR, KEYS), jnp.bfloat16),
            pltpu.VMEM((CHUNK // PAIR, PAIR, TILE), jnp.float32),
            dma, dma((UNITS,)), dma, dma((2,)), dma, dma((12,)),
            dma((UNITS,)), dma((HEADS,)), dma, dma, dma((2, UNITS)), dma((2, UNITS)),
        ],
        compiler_params=pltpu.CompilerParams(
            collective_id=0, has_side_effects=True, vmem_limit_bytes=56 * 1024 * 1024
        ),
    )(query_rows, key_rows, value_rows, block_mask, head_type)


def solution(mesh):
    placed = (
        P(("ctx", "head"), None),
        P(("ctx", "head"), None),
        P(("ctx", "head"), None),
        P("head", "ctx", None),
        P("head"),
    )
    return jax.shard_map(
        per_device, mesh=mesh, in_specs=placed, out_specs=P(("ctx", "head"), None), check_vma=False
    )
```

```python
import math

import jax
import jax.numpy as jnp
from jax import lax
from jax.experimental import pallas as pl
from jax.experimental.pallas import tpu as pltpu
from jax.sharding import PartitionSpec as P

MESH = pl.DeviceIdType.MESH
TILE = 128
DIM = 128
HEADS = 5
ROWS = 96
CHUNK = 768
TILES = CHUNK // TILE
REACH = 12
NEAR = 3
PAIR = 2 * TILE
SPAN = 2 * REACH + 2
KEYS = SPAN * TILE
STEP = 256
UNITS = 2 * HEADS
PIECES = 3 * HEADS
FIRST = 2
LAG_ON, LAG_ACROSS = 1, 3
LAG_ATTEND, TURN = 2, 1
LEAD = 10
WINDOW = 5 * CHUNK
OWN = 2 * CHUNK
CHUNKS = 32
RING = 4
FLAG_ROWS = 16
COUNT = 192
LOW = 1e30
RATE = math.log2(math.e) / math.sqrt(DIM)


def wait_for(ref, sem):
    pltpu.make_async_copy(ref, ref, sem).wait()


def kernel(
    q_ref, k_ref, v_ref, mask_ref, type_ref, o_ref,
    kv, qb, ob, masks, lines, shown, flags, bias, held, weights, totals,
    mask_copy, kv_send, q_send, flag_send, o_send, y_send,
    kv_recv, q_recv, flag_recv, o_recv, near_recv, far_recv,
):
    hd = lax.axis_index("head")
    ctx = lax.axis_index("ctx")
    zh = ctx // 32
    xy = (ctx // 2) % 16
    core = ctx % 2
    z = zh * 4 + hd
    chunk = core * 16 + xy
    loops = zh == core
    has_left = chunk > 0
    has_right = chunk < CHUNKS - 1

    def at(z_, xy_, core_):
        return {"head": z_ % 4, "ctx": (z_ // 4) * 32 + xy_ * 2 + core_}

    def beside(by):
        other = (chunk + by + CHUNKS) % CHUNKS
        return at(z, other % 16, other // 16)

    left, right = beside(-1), beside(1)
    back, ahead = beside(-RING), beside(RING)
    y = xy % RING
    first_row = chunk < RING
    last_row = chunk >= CHUNKS - RING
    at_start, at_end = y == 0, y == RING - 1
    inside = jnp.logical_not(jnp.logical_or(at_start, at_end))
    closing = beside(jnp.where(at_start, RING - 1, 1 - RING))

    barrier = pltpu.get_barrier_semaphore()

    def greet(n, carry):
        other = (z * 2 + core + n) % 16
        pl.semaphore_signal(barrier, inc=1, device_id=at(other // 2, xy, other % 2), device_id_type=MESH)
        return carry

    lax.fori_loop(1, 16, greet, 0)

    has_back, has_ahead = jnp.logical_not(first_row), jnp.logical_not(last_row)
    has_closing = jnp.logical_not(inside)
    partners = ((has_left, left), (has_right, right), (has_back, back), (has_ahead, ahead), (has_closing, closing))
    for there, partner in partners:

        @pl.when(there)
        def _():
            pl.semaphore_signal(barrier, inc=1, device_id=partner, device_id_type=MESH)

    pl.semaphore_wait(barrier, 15 + sum(there.astype(jnp.int32) for there, _ in partners))

    mine = core * 384 + hd * ROWS

    fetch = pltpu.make_async_copy(mask_ref, masks, mask_copy)
    fetch.start()

    def parts(i, z_):
        cols = pl.ds(pl.multiple_of((z_ * HEADS + i) * DIM, DIM), DIM)
        rows = pl.ds(pl.multiple_of(OWN + mine, 16), ROWS)
        q_rows = pl.ds(pl.multiple_of(mine, 16), ROWS)
        return (
            (k_ref.at[:, cols], kv.at[2 * i, rows, :], kv_send.at[2 * i], kv_recv.at[2 * i]),
            (v_ref.at[:, cols], kv.at[2 * i + 1, rows, :], kv_send.at[2 * i + 1], kv_recv.at[2 * i + 1]),
            (q_ref.at[:, cols], qb.at[i, q_rows, :], q_send, q_recv.at[i]),
        )

    def push(src, dst, send, recv, to):
        pltpu.make_async_remote_copy(
            src_ref=src, dst_ref=dst, send_sem=send, recv_sem=recv, device_id=to, device_id_type=MESH
        ).start()

    def spread(i, kind):
        def one(j, carry):
            half = j // 2 + 1
            step = jnp.where(j % 2 == 0, half, 8 - half)
            z_ = (z + step) % 8
            src, dst, send, recv = parts(i, z_)[kind]
            push(src, dst, send, recv, at(z_, xy, zh))
            return carry

        lax.fori_loop(0, 7, one, 0)

        @pl.when(loops)
        def _():
            src, dst, send, recv = parts(i, z)[kind]
            pltpu.make_async_copy(src, dst, recv).start()

        @pl.when(jnp.logical_not(loops))
        def _():
            src, dst, send, recv = parts(i, z)[kind]
            push(src, dst, send, recv, at(z, xy, zh))

    def issue(n, carry):
        late = n - 6
        turn, third = late // 3, late % 3
        i = jnp.where(n < 6, n // 2, jnp.where(n < 12, jnp.where(third == 0, turn, turn + 3), n - 10))
        kind = jnp.where(n < 6, n % 2, jnp.where(jnp.logical_and(n < 12, third > 0), third - 1, 2))
        for option in range(3):

            @pl.when(kind == option)
            def _():
                spread(i, option)

        return carry

    def left_here(u):
        @pl.when(loops)
        def _():
            wait_for(kv.at[u, pl.ds(0, CHUNK - ROWS), :], kv_send.at[u])

        @pl.when(jnp.logical_not(loops))
        def _():
            wait_for(kv.at[u, pl.ds(0, CHUNK), :], kv_send.at[u])

    issue(0, 0)
    left_here(0)
    lax.fori_loop(1, FIRST, issue, 0)

    fetch.wait()
    lines[...] = jnp.zeros_like(lines)
    for h in range(2 * HEADS):
        row = (h // HEADS) * FLAG_ROWS + (h % HEADS) * 3
        lines[pl.ds(row, 3), pl.ds(0, COUNT)] = jnp.where(masks[h] == 1, 1.0, 0.0)
    shape = (2 * FLAG_ROWS, TILE)
    row = lax.broadcasted_iota(jnp.int32, shape, 0)
    third = (row % FLAG_ROWS) % 3
    head_ = (row // FLAG_ROWS) * HEADS + (row % FLAG_ROWS) // 3
    limit = jnp.full(shape, NEAR, jnp.int32)
    for h in range(2 * HEADS):
        limit = jnp.where(jnp.logical_and(head_ == h, type_ref[h] == 1), REACH, limit)
    allowed = jnp.zeros(shape, jnp.float32)
    pick_row = lax.broadcasted_iota(jnp.int32, (lines.shape[1], TILE), 0)
    pick_col = lax.broadcasted_iota(jnp.int32, (lines.shape[1], TILE), 1)
    col = lax.broadcasted_iota(jnp.int32, shape, 1)
    for t in range(3):
        shift = (ctx + t) % 2
        pick = (pick_row - pick_col == 3 * ctx + t - shift - REACH).astype(jnp.bfloat16)
        seen = jnp.dot(lines[...].astype(jnp.bfloat16), pick, preferred_element_type=jnp.float32)
        distance = jnp.abs(col - shift - REACH)
        seen = jnp.where(distance == 0, 1.0, jnp.where(distance <= limit, seen, 0.0))
        allowed = jnp.where(third == t, seen, allowed)
    for e in range(2):
        shown[e] = allowed[e * FLAG_ROWS : (e + 1) * FLAG_ROWS]

    for e in range(2):
        z_ = 2 * hd + e
        here = jnp.logical_and(loops, z_ == z)

        @pl.when(here)
        def _():
            pltpu.make_async_copy(shown.at[e], flags.at[core], flag_recv).start()

        @pl.when(jnp.logical_not(here))
        def _():
            push(shown.at[e], flags.at[core], flag_send.at[e], flag_recv, at(z_, xy, zh))

    def clear(slot, when):
        @pl.when(when)
        def _():
            def one(i, carry):
                kv[i, pl.ds(slot * CHUNK, CHUNK), :] = jnp.zeros((CHUNK, DIM), jnp.bfloat16)
                return carry

            lax.fori_loop(0, UNITS, one, 0)

    clear(0, chunk < 2)
    clear(1, chunk < 1)
    clear(3, chunk > CHUNKS - 2)
    clear(4, chunk > CHUNKS - 3)

    def slot(i, s):
        return kv.at[i, pl.ds(s * CHUNK, CHUNK), :]

    def send_own(i):
        wait_for(slot(i, 2), kv_recv.at[i])

        @pl.when(has_right)
        def _():
            push(slot(i, 2), slot(i, 1), y_send.at[0], near_recv.at[0, i], right)

        @pl.when(has_left)
        def _():
            push(slot(i, 2), slot(i, 3), y_send.at[1], near_recv.at[1, i], left)

    def both(*terms):
        out = terms[0]
        for term in terms[1:]:
            out = jnp.logical_and(out, term)
        return out

    def either(one, other):
        return jnp.logical_or(one, other)

    to_right = (both(inside, has_left), both(has_left, either(at_start, both(y == 1, first_row))))
    to_left = (both(inside, has_right), both(has_right, either(at_end, both(y == 2, last_row))))
    left_closes = both(at_end, has_left)
    right_closes = both(at_start, has_right)
    high_first = (y < 2, y % 2 == 0)
    has_low, has_high = chunk >= 2, chunk < CHUNKS - 2

    def pass_on(u, kind):
        @pl.when(has_left)
        def _():
            wait_for(slot(u, 1), near_recv.at[0, u])

        @pl.when(to_right[kind])
        def _():
            push(slot(u, 1), slot(u, 0), y_send.at[2 + kind], far_recv.at[0, u], right)

        if kind == 1:

            @pl.when(left_closes)
            def _():
                push(slot(u, 1), slot(u, 4), y_send.at[6], far_recv.at[1, u], closing)

        @pl.when(has_right)
        def _():
            wait_for(slot(u, 3), near_recv.at[1, u])

        @pl.when(to_left[kind])
        def _():
            push(slot(u, 3), slot(u, 4), y_send.at[4 + kind], far_recv.at[1, u], left)

        if kind == 1:

            @pl.when(right_closes)
            def _():
                push(slot(u, 3), slot(u, 0), y_send.at[7], far_recv.at[0, u], closing)

    def pass_across(u, kind):
        high = high_first[kind]

        @pl.when(both(high, has_high))
        def _():
            wait_for(slot(u, 4), far_recv.at[1, u])

        @pl.when(both(high, has_ahead))
        def _():
            push(slot(u, 4), slot(u, 0), y_send.at[8 + kind], far_recv.at[0, u], ahead)

        @pl.when(both(jnp.logical_not(high), has_low))
        def _():
            wait_for(slot(u, 0), far_recv.at[0, u])

        @pl.when(both(jnp.logical_not(high), has_back))
        def _():
            push(slot(u, 0), slot(u, 4), y_send.at[10 + kind], far_recv.at[1, u], back)

    def see():
        wait_for(flags, flag_recv)
        spots = lax.broadcasted_iota(jnp.int32, (TILE, KEYS), 1) // TILE
        rows_ = lax.broadcasted_iota(jnp.int32, (TILE, KEYS), 0)
        wide = (spots == rows_).astype(jnp.bfloat16)
        for c in range(2):
            seen = jnp.dot(flags[c].astype(jnp.bfloat16), wide, preferred_element_type=jnp.float32)
            seen = (seen - 1.0) * LOW
            for i in range(HEADS):
                bias[pl.ds(i * TILES + 3 * c, 3), :] = seen[3 * i : 3 * i + 3]

    def attend(i):
        def arrived(u, kind):
            @pl.when(both(high_first[kind], has_low))
            def _():
                wait_for(slot(u, 0), far_recv.at[0, u])

            @pl.when(both(jnp.logical_not(high_first[kind]), has_high))
            def _():
                wait_for(slot(u, 4), far_recv.at[1, u])

        wait_for(qb.at[i], q_recv.at[i])
        arrived(2 * i, 0)
        for p in range(CHUNK // PAIR):
            start = p * PAIR
            q = qb[i, pl.ds(start, PAIR), :]
            best = jnp.full((PAIR, TILE), -3e38, jnp.float32)
            for j in range(0, KEYS, STEP):
                keys = kv[2 * i, pl.ds(start + j, STEP), :]
                s = lax.dot_general(q, keys, (((1,), (1,)), ((), ())), preferred_element_type=jnp.float32)
                even = s[:TILE] + bias[pl.ds(i * TILES + 2 * p, 1), pl.ds(j, STEP)]
                odd = s[TILE:] + bias[pl.ds(i * TILES + 2 * p + 1, 1), pl.ds(j, STEP)]
                s = jnp.concatenate([even, odd], axis=0)
                held[p, :, pl.ds(j, STEP)] = s
                for t in range(0, STEP, TILE):
                    best = jnp.maximum(best, s[:, t : t + TILE])
            best = jnp.max(best, axis=1, keepdims=True)
            total = jnp.zeros((PAIR, TILE), jnp.float32)
            for j in range(0, KEYS, STEP):
                raw = jnp.exp2((held[p, :, pl.ds(j, STEP)] - best) * RATE)
                for t in range(0, STEP, TILE):
                    total = total + raw[:, t : t + TILE]
                weights[p, :, pl.ds(j, STEP)] = raw.astype(jnp.bfloat16)
            totals[p] = jnp.broadcast_to(jnp.sum(total, axis=1, keepdims=True), (PAIR, TILE))

        arrived(2 * i + 1, 1)
        for p in range(CHUNK // PAIR):
            start = p * PAIR
            values = kv[2 * i + 1, pl.ds(start, KEYS), :]
            mixed = jnp.dot(weights[p], values, preferred_element_type=jnp.float32)
            ob[i, pl.ds(start, PAIR), :] = (mixed / totals[p]).astype(jnp.bfloat16)

        cols = pl.ds(pl.multiple_of((z * HEADS + i) * DIM, DIM), DIM)

        def owner(n):
            zl = (hd + n // 2) % 4
            cs = (core + n) % 2
            return ob.at[i, pl.ds(pl.multiple_of(cs * 384 + zl * ROWS, 16), ROWS), :], at(core * 4 + zl, xy, cs)

        @pl.when(loops)
        def _():
            pltpu.make_async_copy(owner(0)[0], o_ref.at[:, cols], o_recv).start()

        @pl.when(jnp.logical_not(loops))
        def _():
            push(owner(0)[0], o_ref.at[:, cols], o_send, o_recv, owner(0)[1])

        def one(n, carry):
            src, to = owner(n)
            push(src, o_ref.at[:, cols], o_send, o_recv, to)
            return carry

        lax.fori_loop(1, 8, one, 0)

    def within(n, count):
        return jnp.logical_and(n >= 0, n < count)

    def advance(s, carry):
        for t in range(2):
            u = 2 * s + t

            @pl.when(u < UNITS)
            def _():
                send_own(u)
                low = jnp.where(u == 0, FIRST, jnp.minimum(PIECES, LEAD + 2 * u - 2))
                lax.fori_loop(low, jnp.minimum(PIECES, LEAD + 2 * u), issue, 0)

            @pl.when(within(u - LAG_ON, UNITS))
            def _():
                pass_on(u - LAG_ON, (t - LAG_ON) % 2)

            @pl.when(within(u - LAG_ACROSS, UNITS))
            def _():
                pass_across(u - LAG_ACROSS, (t - LAG_ACROSS) % 2)

            if t == TURN:

                @pl.when(s == 0)
                def _():
                    see()

                @pl.when(within(s - LAG_ATTEND, HEADS))
                def _():
                    attend(s - LAG_ATTEND)

        return carry

    lax.fori_loop(0, HEADS + LAG_ATTEND, advance, 0)

    wait_for(o_ref, o_recv)

    def sent(rows):
        wait_for(qb.at[:, pl.ds(0, rows), :], q_send)
        wait_for(ob.at[:, pl.ds(0, rows), :], o_send)

    @pl.when(loops)
    def _():
        sent(CHUNK - ROWS)

    @pl.when(jnp.logical_not(loops))
    def _():
        sent(CHUNK)

    def drain(u, carry):
        left_here(u)
        return carry

    lax.fori_loop(1, UNITS, drain, 0)

    for e in range(2):

        @pl.when(jnp.logical_not(jnp.logical_and(loops, 2 * hd + e == z)))
        def _():
            wait_for(shown.at[e], flag_send.at[e])

    gone = [(has_right, 0, UNITS), (has_left, 1, UNITS), (left_closes, 6, HEADS), (right_closes, 7, HEADS)]
    for kind in range(2):
        gone += [(to_right[kind], 2 + kind, HEADS), (to_left[kind], 4 + kind, HEADS)]
        gone += [(both(high_first[kind], has_ahead), 8 + kind, HEADS)]
        gone += [(both(jnp.logical_not(high_first[kind]), has_back), 10 + kind, HEADS)]
    for there, which, units in gone:

        @pl.when(there)
        def _():
            wait_for(kv.at[pl.ds(0, units), pl.ds(0, CHUNK), :], y_send.at[which])


def per_device(query_rows, key_rows, value_rows, block_mask, head_type):
    any_ = pl.BlockSpec(memory_space=pltpu.HBM)
    dma = pltpu.SemaphoreType.DMA
    return pl.pallas_call(
        kernel,
        out_shape=pltpu.VMEM(query_rows.shape, jnp.bfloat16),
        in_specs=[any_] * 4 + [pl.BlockSpec(memory_space=pltpu.SMEM)],
        out_specs=pl.BlockSpec(memory_space=pl.ANY),
        scratch_shapes=[
            pltpu.VMEM((UNITS, WINDOW, DIM), jnp.bfloat16),
            pltpu.VMEM((HEADS, CHUNK, DIM), jnp.bfloat16),
            pltpu.VMEM((HEADS, CHUNK, DIM), jnp.bfloat16),
            pltpu.VMEM(block_mask.shape, jnp.int32),
            pltpu.VMEM((2 * FLAG_ROWS, 2 * TILE), jnp.float32),
            pltpu.VMEM((2, FLAG_ROWS, TILE), jnp.float32),
            pltpu.VMEM((2, FLAG_ROWS, TILE), jnp.float32),
            pltpu.VMEM((HEADS * TILES + 2, KEYS), jnp.float32),
            pltpu.VMEM((CHUNK // PAIR, PAIR, KEYS), jnp.float32),
            pltpu.VMEM((CHUNK // PAIR, PAIR, KEYS), jnp.bfloat16),
            pltpu.VMEM((CHUNK // PAIR, PAIR, TILE), jnp.float32),
            dma, dma((UNITS,)), dma, dma((2,)), dma, dma((12,)),
            dma((UNITS,)), dma((HEADS,)), dma, dma, dma((2, UNITS)), dma((2, UNITS)),
        ],
        compiler_params=pltpu.CompilerParams(
            collective_id=0, has_side_effects=True, vmem_limit_bytes=56 * 1024 * 1024
        ),
    )(query_rows, key_rows, value_rows, block_mask, head_type)


def solution(mesh):
    placed = (
        P(("ctx", "head"), None),
        P(("ctx", "head"), None),
        P(("ctx", "head"), None),
        P("head", "ctx", None),
        P("head"),
    )
    return jax.shard_map(
        per_device, mesh=mesh, in_specs=placed, out_specs=P(("ctx", "head"), None), check_vma=False
    )
```
